32 devices in a mesh: seq: 8 (over y, x, core), head: 4 (over z).
Axes of the slice: x: 2, y: 2, z: 4, core: 2. Of those that a mesh axis runs over, the one named last changes fastest.
Arguments:
- queries: bfloat16 [16384, 8192], P('seq', 'head'), may hold values from -6 to 6
- key_vectors: bfloat16 [16384, 8192], P('seq', 'head'), may hold values from -6 to 6
- value_vectors: bfloat16 [16384, 8192], P('seq', 'head'), may hold values from -6 to 6
- level_weights: float32 [64, 16, 16384], P('head', None, 'seq'), may hold values from 0.22 to 13.45, as said below
- norm_gain: float32 [8192], P('head'), may hold values from 0.25 to 1.75
Outputs:
- normed: bfloat16 [16384, 8192], P('seq', 'head')
The draws below stay inside these ranges and needn't reach their ends.
Inputs may be any that keep to these rules, and one draw needn't show every extreme that they name: `level_weights`: positive.
All inputs are finite; a program needn't handle non-finite values.
Results may differ from the reference program's by a relative error of at most 0.0056.
Values may be sent and summed in bfloat16 or wider, within the bound.
No kernel may reach another device: no remote copies, remote signals or barrier semaphores. Data moves between devices by JAX's collectives and lax.ppermute only.
A program may use at most 256 MiB of HBM per device.

```python
import jax
import jax.numpy as jnp
from jax import lax

HEADS = 64
HEAD_DIM = 128
VALUE_DIM = 128
LEVELS = 16
TOK_DEV = 2048
TOKENS = 16384


def draw_level_weights(key, part):
    uniform_draw = jax.random.uniform(key, (HEADS, LEVELS, TOKENS), jnp.float32)
    head_factor = 3.0 ** (jnp.arange(HEADS, dtype=jnp.float32) / (HEADS - 1))
    base_values = jnp.exp(-1.5 + 3.0 * uniform_draw)
    return base_values * head_factor[:, None, None]


def level_of(stream_key, shape, cuts, least, largest):
    def one(position, parts):
        heights = jax.random.uniform(jax.random.fold_in(jax.random.fold_in(stream_key, 6), position), (parts,), jnp.float32, least / len(cuts), largest / len(cuts))
        return jnp.repeat(jnp.exp(heights), shape[position] // parts).reshape((-1,) + (1,) * (len(shape) - position - 1))

    loudness = one(*cuts[0])
    for cut in cuts[1:]:
        loudness = loudness * one(*cut)
    return loudness


def normal_values(key, dims, deviation, most, split=(), held_as=jnp.bfloat16):
    array = deviation * jax.random.normal(key, dims, jnp.float32)
    if split:
        array = array * level_of(key, dims, split, -0.22, 0.18)
    return jnp.clip(array, -most, most).astype(held_as)


def setup_inputs(seed: int = 0) -> dict:
    key_of = jax.random.split(jax.random.key(seed), 6)
    return {
        "queries": normal_values(key_of[0], (TOKENS, HEADS * HEAD_DIM), 1.0, 6.0, ((0, 8), (1, 4))),
        "key_vectors": normal_values(key_of[1], (TOKENS, HEADS * HEAD_DIM), 1.0, 6.0, ((0, 8), (1, 4))),
        "value_vectors": normal_values(key_of[2], (TOKENS, HEADS * VALUE_DIM), 1.0, 6.0, ((0, 8), (1, 4))),
        "level_weights": draw_level_weights(jax.random.fold_in(key_of[5], 71), 0),
        "norm_gain": jnp.clip(1.0 + 0.15 * jax.random.normal(key_of[4], (HEADS * VALUE_DIM,), jnp.float32), 0.25, 1.75),
    }


def bit_length(numbers, count):
    counted = jnp.zeros(numbers.shape, jnp.int32)
    for exponent in range(count):
        counted = counted + (numbers >= 1 << exponent).astype(jnp.int32)
    return counted

def one_head(operands):
    query, key_rows, value_rows, weights = operands
    block_count = TOKENS // TOK_DEV
    scaling = HEAD_DIM ** (-0.5)
    local_bits = TOK_DEV.bit_length() - 1
    cross_bits = block_count.bit_length() - 1
    query_blocks = query.astype(jnp.float32).reshape(block_count, TOK_DEV, HEAD_DIM)
    key_blocks = key_rows.astype(jnp.float32).reshape(block_count, TOK_DEV, HEAD_DIM)
    value_blocks = value_rows.astype(jnp.float32).reshape(block_count, TOK_DEV, VALUE_DIM)
    weight_blocks = weights.reshape(LEVELS, block_count, TOK_DEV)
    row_block = min(TOK_DEV, 512)
    pieces = []
    for start_row in range(0, TOK_DEV, row_block):
        end_row = start_row + row_block
        row_ids = jnp.arange(start_row, end_row, dtype=jnp.int32)
        col_ids = jnp.arange(0, end_row, dtype=jnp.int32)
        levels = bit_length(row_ids[:, None] ^ col_ids[None, :], local_bits)
        scores = jnp.einsum('crd,csd->crs', query_blocks[:, start_row:end_row], key_blocks[:, :end_row]) * scaling
        factors = jnp.zeros(scores.shape, jnp.float32)
        for depth_id in range(local_bits + 1):
            factors = jnp.where(levels[None] == depth_id, weight_blocks[depth_id, :, start_row:end_row][:, :, None], factors)
        causal = (col_ids[None, :] <= row_ids[:, None])[None]
        weighted = jnp.where(causal, scores * factors, 0.0).astype(jnp.bfloat16)
        pieces.append(jnp.einsum('crs,cse->cre', weighted.astype(jnp.float32), value_blocks[:, :end_row]))
    inside = jnp.concatenate(pieces, axis=1)
    states = jnp.einsum('ctd,cte->cde', key_blocks, value_blocks)
    states = lax.optimization_barrier(states.astype(jnp.bfloat16)).astype(jnp.float32)
    prefix = jnp.concatenate([jnp.zeros((1, HEAD_DIM, VALUE_DIM), jnp.float32), jnp.cumsum(states, axis=0)], axis=0)
    block_ids = jnp.arange(block_count, dtype=jnp.int32)
    across = jnp.zeros((block_count, TOK_DEV, VALUE_DIM), jnp.float32)
    for bit_level in range(cross_bits):
        lower = block_ids >> bit_level + 1 << bit_level + 1
        upper = lower + (1 << bit_level)
        present = (block_ids >> bit_level & 1).astype(jnp.float32)
        bucket = (prefix[upper] - prefix[lower]) * present[:, None, None]
        rounded = lax.optimization_barrier(bucket.astype(jnp.bfloat16))
        readout = jnp.einsum('ctd,cde->cte', query_blocks, rounded.astype(jnp.float32)) * scaling
        across = across + weight_blocks[local_bits + 1 + bit_level][:, :, None] * readout
    return (inside + across).reshape(TOKENS, VALUE_DIM)

def reference(queries, key_vectors, value_vectors, level_weights, norm_gain):
    query_heads = queries.reshape(TOKENS, HEADS, HEAD_DIM).transpose(1, 0, 2)
    key_heads = key_vectors.reshape(TOKENS, HEADS, HEAD_DIM).transpose(1, 0, 2)
    value_heads = value_vectors.reshape(TOKENS, HEADS, VALUE_DIM).transpose(1, 0, 2)
    outputs = lax.map(one_head, (query_heads, key_heads, value_heads, level_weights))
    mixture = outputs.transpose(1, 0, 2).reshape(TOKENS, HEADS * VALUE_DIM)
    square = lax.optimization_barrier(jnp.sum(mixture * mixture, axis=1, keepdims=True))
    return (mixture * norm_gain * lax.rsqrt(square / (HEADS * VALUE_DIM) + 1e-05)).astype(jnp.bfloat16)
```

```python
import functools

import jax
import jax.numpy as jnp
from jax import lax
from jax.experimental import pallas as pl
from jax.experimental.pallas import tpu as pltpu
from jax.sharding import PartitionSpec as P

HEADS = 64
HEAD_DIM = 128
VALUE_DIM = 128
CHUNK = 256
HALF = 128
GROUP = 8
B_PARTS = 4
C_PARTS = 2
SCALING = HEAD_DIM ** (-0.5)

TT = (((1,), (1,)), ((), ()))
LT = (((0,), (0,)), ((), ()))
NN = (((1,), (0,)), ((), ()))


def dot(a, b, dims):
    return lax.dot_general(a, b, dims, preferred_element_type=jnp.float32)


def bucket_slot(depth_count, depth, chunk):
    before = sum(1 << (depth_count - d - 1) for d in range(depth))
    return before + (((chunk >> depth) - 1) >> 1)


def state_kernel(k_ref, v_ref, local_ref, block_ref):
    rows = k_ref.shape[0]
    chunks = rows // CHUNK
    depth_count = chunks.bit_length() - 1
    sums = []
    for c in range(chunks):
        here = pl.ds(c * CHUNK, CHUNK)
        sums.append(dot(v_ref[here, :], k_ref[here, :], LT))
    slot = 0
    for _ in range(depth_count):
        for m in range(0, len(sums), 2):
            local_ref[0, slot] = sums[m].astype(jnp.bfloat16)
            slot += 1
        sums = [sums[m] + sums[m + 1] for m in range(0, len(sums), 2)]
    block_ref[0] = sums[0].astype(jnp.bfloat16)


def local_factors(w_ref, start):
    def row(level):
        return w_ref[0, level : level + 1, start : start + HALF] * SCALING

    groups = HALF // GROUP
    group_id = lax.broadcasted_iota(jnp.int32, (groups, HALF), 0)
    lane_group = lax.broadcasted_iota(jnp.int32, (groups, HALF), 1) >> 3
    apart = group_id ^ lane_group
    coarse = jnp.broadcast_to(row(4), (groups, HALF))
    for level in range(5, 8):
        coarse = jnp.where(apart >= 1 << (level - 4), row(level), coarse)
    coarse = jnp.where(lane_group > group_id, coarse, 0.0)
    sub = lax.broadcasted_iota(jnp.int32, (GROUP, HALF), 0)
    lane = lax.broadcasted_iota(jnp.int32, (GROUP, HALF), 1)
    low = sub ^ (lane & 7)
    fine = jnp.broadcast_to(row(0), (GROUP, HALF))
    for level in range(1, 4):
        fine = jnp.where(low >= 1 << (level - 1), row(level), fine)
    fine = jnp.where(sub <= (lane & 7), fine, 0.0)
    pieces = []
    for g in range(groups):
        wide = jnp.broadcast_to(coarse[g : g + 1, :], (GROUP, HALF))
        pieces.append(jnp.where(lane >> 3 == g, fine, wide))
    return jnp.concatenate(pieces, axis=0)


def local_kernel(*refs):
    q_ref, k_ref, v_ref, w_ref, local_ref = refs[:5]
    out_ref = refs[-1]
    rows = q_ref.shape[0]
    chunks = rows // CHUNK
    depth_count = chunks.bit_length() - 1
    base_level = CHUNK.bit_length()
    for c in range(chunks):
        start = c * CHUNK
        here = pl.ds(start, CHUNK)
        q = q_ref[here, :]
        depths = [d for d in range(depth_count) if c >> d & 1]
        stream = [k_ref[here, :]] + [
            local_ref[0, bucket_slot(depth_count, d, c)] for d in depths
        ]
        result = dot(jnp.concatenate(stream, axis=0), q, TT)
        upper = (result[:HALF, :HALF] * local_factors(w_ref, start)).astype(jnp.bfloat16)
        lower = (result[HALF:CHUNK, HALF:] * local_factors(w_ref, start + HALF)).astype(
            jnp.bfloat16
        )
        middle_row = w_ref[0, 8:9, start + HALF : start + CHUNK] * SCALING
        middle = (result[:HALF, HALF:] * middle_row).astype(jnp.bfloat16)
        weighted = jnp.concatenate(
            [
                jnp.concatenate([upper, middle], axis=1),
                jnp.concatenate([jnp.zeros_like(upper), lower], axis=1),
            ],
            axis=0,
        )
        total = dot(v_ref[here, :], weighted, LT)
        for i, d in enumerate(depths):
            piece = result[CHUNK + i * VALUE_DIM : CHUNK + (i + 1) * VALUE_DIM]
            level = base_level + d
            total += piece * (w_ref[0, level : level + 1, start : start + CHUNK] * SCALING)
        out_ref[0, :, start : start + CHUNK] = total.astype(out_ref.dtype)


def across_kernel(cross_bits, half_heads, first_level, pos_ref, q_ref, w_ref, in_ref, *refs):
    mix_ref, square_ref = refs[-2:]
    state_refs = refs[: 2 * cross_bits - 1]
    head = pl.program_id(0)
    position = pos_ref[0]
    states = []
    for b in range(cross_bits):
        if b == 0:
            state = state_refs[0][0]
        else:
            own = (head // half_heads) == (position & 1)
            state = jnp.where(own, state_refs[2 * b - 1][0], state_refs[2 * b][0])
        present = (position >> b & 1) == 1
        states.append(jnp.where(present, state, jnp.zeros_like(state)))
    stream = jnp.concatenate(states, axis=0)
    rows = q_ref.shape[0]

    @pl.when(head == 0)
    def _():
        square_ref[...] = jnp.zeros_like(square_ref)

    for start in range(0, rows, CHUNK):
        result = dot(stream, q_ref[start : start + CHUNK, :], TT)
        total = in_ref[0, :, start : start + CHUNK].astype(jnp.float32)
        for b in range(cross_bits):
            level = first_level + b
            total += result[b * VALUE_DIM : (b + 1) * VALUE_DIM] * (
                w_ref[0, level : level + 1, start : start + CHUNK] * SCALING
            )
        square_ref[:, start : start + CHUNK] += jnp.sum(total * total, axis=0, keepdims=True)
        mix_ref[start : start + CHUNK, :] = total.T.astype(mix_ref.dtype)


def norm_kernel(width, mix_ref, gain_ref, square_ref, *refs):
    out_ref = refs[-1]
    rows = mix_ref.shape[0]
    factor = lax.rsqrt(square_ref[...] / width + 1e-05)
    column = jnp.broadcast_to(factor, (GROUP, rows)).T[:, :1]
    out_ref[...] = (mix_ref[...].astype(jnp.float32) * gain_ref[...] * column).astype(
        out_ref.dtype
    )


def body(queries, key_vectors, value_vectors, level_weights, norm_gain):
    rows = queries.shape[0]
    heads = level_weights.shape[0]
    levels = level_weights.shape[1]
    chunks = rows // CHUNK
    depth_count = chunks.bit_length() - 1
    local_bits = rows.bit_length() - 1
    seq_size = lax.axis_size("seq")
    cross_bits = seq_size.bit_length() - 1
    position = lax.axis_index("seq").astype(jnp.int32)
    bf16 = jnp.bfloat16

    head_block = pl.BlockSpec((rows, HEAD_DIM), lambda h: (0, h))
    local_states, block_state = pl.pallas_call(
        state_kernel,
        grid=(heads,),
        in_specs=[head_block, head_block],
        out_specs=[
            pl.BlockSpec((1, chunks - 1, VALUE_DIM, HEAD_DIM), lambda h: (h, 0, 0, 0)),
            pl.BlockSpec((1, VALUE_DIM, HEAD_DIM), lambda h: (h, 0, 0)),
        ],
        out_shape=[
            jax.ShapeDtypeStruct((heads, chunks - 1, VALUE_DIM, HEAD_DIM), bf16),
            jax.ShapeDtypeStruct((heads, VALUE_DIM, HEAD_DIM), bf16),
        ],
        cost_estimate=pl.CostEstimate(
            flops=2 * heads * rows * HEAD_DIM * VALUE_DIM,
            bytes_accessed=4 * rows * heads * HEAD_DIM,
            transcendentals=0,
        ),
        name="states",
    )(key_vectors, value_vectors)

    def swap(array, bit):
        return lax.ppermute(array, "seq", [(i, i ^ (1 << bit)) for i in range(seq_size)])

    half = heads // 2
    buckets = []
    received = swap(block_state, 0)
    buckets.append(received)
    if cross_bits > 1:
        first = (position & 1) * half
        mine = lax.dynamic_slice_in_dim(block_state, first, half, 0)
        pair = lax.dynamic_slice_in_dim(received, first, half, 0)
        running = (mine.astype(jnp.float32) + pair.astype(jnp.float32)).astype(bf16)
        for b in range(1, cross_bits):
            received = swap(running, b)
            buckets += [received, swap(received, 0)]
            running = (running.astype(jnp.float32) + received.astype(jnp.float32)).astype(bf16)

    part = heads // B_PARTS
    inside = None
    for p in range(B_PARTS):
        block = pl.BlockSpec((rows, HEAD_DIM), lambda h, p=p: (0, h + p * part))
        operands = [queries, key_vectors, value_vectors, level_weights, local_states]
        in_specs = [
            block,
            block,
            block,
            pl.BlockSpec((1, levels, rows), lambda h, p=p: (h + p * part, 0, 0)),
            pl.BlockSpec(
                (1, chunks - 1, VALUE_DIM, HEAD_DIM), lambda h, p=p: (h + p * part, 0, 0, 0)
            ),
        ]
        aliases = {}
        if inside is not None:
            operands.append(inside)
            in_specs.append(pl.BlockSpec(memory_space=pl.ANY))
            aliases = {5: 0}
        inside = pl.pallas_call(
            local_kernel,
            grid=(part,),
            in_specs=in_specs,
            out_specs=pl.BlockSpec((1, VALUE_DIM, rows), lambda h, p=p: (h + p * part, 0, 0)),
            out_shape=jax.ShapeDtypeStruct((heads, VALUE_DIM, rows), bf16),
            input_output_aliases=aliases,
            cost_estimate=pl.CostEstimate(
                flops=part * rows * HEAD_DIM * 16 * 256,
                bytes_accessed=8 * rows * part * HEAD_DIM,
                transcendentals=0,
            ),
            name="local",
        )(*operands)

    span = rows // C_PARTS
    first_level = local_bits + 1
    low = first_level // 8 * 8
    count = 8 if (first_level + cross_bits - 1) // 8 * 8 == low else levels
    level_block = low // 8 if count == 8 else 0
    first_level = first_level - low if count == 8 else first_level
    mixes, squares = [], []
    for p in range(C_PARTS):
        operands = [position.reshape(1), queries, level_weights, inside] + buckets
        in_specs = [
            pl.BlockSpec(memory_space=pltpu.SMEM),
            pl.BlockSpec((span, HEAD_DIM), lambda h, p=p: (p, h)),
            pl.BlockSpec((1, count, span), lambda h, p=p: (h, level_block, p)),
            pl.BlockSpec((1, VALUE_DIM, span), lambda h, p=p: (h, 0, p)),
            pl.BlockSpec((1, VALUE_DIM, HEAD_DIM), lambda h: (h, 0, 0)),
        ] + [pl.BlockSpec((1, VALUE_DIM, HEAD_DIM), lambda h: (h % half, 0, 0))] * (
            2 * cross_bits - 2
        )
        mix, square = pl.pallas_call(
            functools.partial(across_kernel, cross_bits, half, first_level),
            grid=(heads,),
            in_specs=in_specs,
            out_specs=[
                pl.BlockSpec((span, VALUE_DIM), lambda h: (0, h)),
                pl.BlockSpec((1, span), lambda h: (0, 0)),
            ],
            out_shape=[
                jax.ShapeDtypeStruct((span, heads * VALUE_DIM), bf16),
                jax.ShapeDtypeStruct((1, span), jnp.float32),
            ],
            cost_estimate=pl.CostEstimate(
                flops=heads * span * HEAD_DIM * 2 * 128 * cross_bits * 4,
                bytes_accessed=6 * span * heads * HEAD_DIM,
                transcendentals=0,
            ),
            name="across",
        )(*operands)
        mixes.append(mix)
        squares.append(lax.psum(square, "head"))

    out = None
    step = 256
    width = HEADS * VALUE_DIM
    gain = norm_gain.reshape(1, -1)
    columns = heads * VALUE_DIM
    for p in range(C_PARTS):
        operands = [mixes[p], gain, squares[p]]
        in_specs = [
            pl.BlockSpec((step, columns), lambda i: (i, 0)),
            pl.BlockSpec((1, columns), lambda i: (0, 0)),
            pl.BlockSpec((1, step), lambda i: (0, i)),
        ]
        aliases = {}
        if out is not None:
            operands.append(out)
            in_specs.append(pl.BlockSpec(memory_space=pl.ANY))
            aliases = {3: 0}
        out = pl.pallas_call(
            functools.partial(norm_kernel, width),
            grid=(span // step,),
            in_specs=in_specs,
            out_specs=pl.BlockSpec((step, columns), lambda i, p=p: (i + p * (span // step), 0)),
            out_shape=jax.ShapeDtypeStruct((rows, columns), bf16),
            input_output_aliases=aliases,
            cost_estimate=pl.CostEstimate(
                flops=3 * span * columns, bytes_accessed=4 * span * columns, transcendentals=0
            ),
            name="norm",
        )(*operands)
    return out


def solution(mesh):
    placed = (
        P("seq", "head"),
        P("seq", "head"),
        P("seq", "head"),
        P("head", None, "seq"),
        P("head"),
    )
    return jax.shard_map(
        body, mesh=mesh, in_specs=placed, out_specs=P("seq", "head"), check_vma=False
    )
```

```python
import functools

import jax
import jax.numpy as jnp
from jax import lax
from jax.experimental import pallas as pl
from jax.experimental.pallas import tpu as pltpu
from jax.sharding import PartitionSpec as P

HEADS = 64
HEAD_DIM = 128
VALUE_DIM = 128
CHUNK = 256
HALF = 128
GROUP = 8
SCALING = HEAD_DIM ** (-0.5)
MIB = 1 << 20
BF16 = jnp.bfloat16

TT = (((1,), (1,)), ((), ()))
LT = (((0,), (0,)), ((), ()))

WHOLE = pl.BlockSpec(memory_space=pltpu.VMEM)
ANYWHERE = pl.BlockSpec(memory_space=pl.ANY)


def dot(a, b, dims):
    return lax.dot_general(a, b, dims, preferred_element_type=jnp.float32)


def keep(array):
    return pltpu.with_memory_space_constraint(array, pltpu.VMEM)


def leave(array):
    return pltpu.with_memory_space_constraint(array, pltpu.HBM)


def columns_of(head):
    if isinstance(head, int):
        return slice(head * HEAD_DIM, (head + 1) * HEAD_DIM)
    return pl.ds(pl.multiple_of(head * HEAD_DIM, HEAD_DIM), HEAD_DIM)


def rows_of(chunk):
    return slice(chunk * CHUNK, (chunk + 1) * CHUNK)


def bucket_slot(depth_count, depth, chunk):
    before = sum(1 << (depth_count - d - 1) for d in range(depth))
    return before + (((chunk >> depth) - 1) >> 1)


def state_kernel(
    span, pos_ref, k_hbm, v_hbm, q_hbm, w_hbm,
    k_ref, v_ref, local_ref, block_ref, q_ref, w_ref, held, sems, more_sems,
):
    del pos_ref
    rows = k_ref.shape[0]
    heads = block_ref.shape[0]
    chunks = rows // CHUNK
    depth_count = chunks.bit_length() - 1
    copies = []
    for c in range(chunks):
        here = pl.ds(c * CHUNK, CHUNK)
        pair = [
            pltpu.make_async_copy(k_hbm.at[here], k_ref.at[here], sems.at[0, c]),
            pltpu.make_async_copy(v_hbm.at[here], v_ref.at[here], sems.at[1, c]),
        ]
        for copy in pair:
            copy.start()
        copies.append(pair)
    more = weight_copies(span, q_hbm, w_hbm, q_ref, w_ref, more_sems)
    for c in range(chunks):
        for copy in copies[c]:
            copy.wait()
        if c == chunks // 2:
            for copy in more:
                copy.start()
        for h in range(heads):
            state = dot(v_ref[rows_of(c), columns_of(h)], k_ref[rows_of(c), columns_of(h)], LT)
            depth = 0
            while c >> depth & 1:
                state += held[depth, h]
                depth += 1
            if depth < depth_count:
                held[depth, h] = state
                slot = bucket_slot(depth_count, depth, c | (1 << depth))
                local_ref[h, slot] = state.astype(BF16)
            else:
                block_ref[h] = state.astype(BF16)
    for copy in more:
        copy.wait()


def weight_copies(span, q_hbm, w_hbm, q_ref, w_ref, sems):
    here = pl.ds(span[0] * CHUNK, (span[1] - span[0]) * CHUNK)
    return [
        pltpu.make_async_copy(w_hbm.at[:, :, here], w_ref, sems.at[0]),
        pltpu.make_async_copy(q_hbm.at[here], q_ref, sems.at[1]),
    ]


def sum_kernel(whole, pos_ref, mine_ref, received_ref, out_ref):
    half = out_ref.shape[0]
    here = pl.ds((pos_ref[0] & 1) * half if whole else 0, half)
    total = mine_ref[here].astype(jnp.float32) + received_ref[here].astype(jnp.float32)
    out_ref[...] = total.astype(BF16)


def local_factors(w_ref, head, start):
    def row(level):
        return w_ref[head, level : level + 1, start : start + HALF] * SCALING

    groups = HALF // GROUP
    group_id = lax.broadcasted_iota(jnp.int32, (groups, HALF), 0)
    lane_group = lax.broadcasted_iota(jnp.int32, (groups, HALF), 1) >> 3
    apart = group_id ^ lane_group
    coarse = jnp.broadcast_to(row(4), (groups, HALF))
    for level in range(5, 8):
        coarse = jnp.where(apart >= 1 << (level - 4), row(level), coarse)
    coarse = jnp.where(lane_group > group_id, coarse, 0.0)
    sub = lax.broadcasted_iota(jnp.int32, (GROUP, HALF), 0)
    lane = lax.broadcasted_iota(jnp.int32, (GROUP, HALF), 1)
    low = sub ^ (lane & 7)
    fine = jnp.broadcast_to(row(0), (GROUP, HALF))
    for level in range(1, 4):
        fine = jnp.where(low >= 1 << (level - 1), row(level), fine)
    fine = jnp.where(sub <= (lane & 7), fine, 0.0)
    pieces = []
    for g in range(groups):
        wide = jnp.broadcast_to(coarse[g : g + 1, :], (GROUP, HALF))
        pieces.append(jnp.where(lane >> 3 == g, fine, wide))
    return jnp.concatenate(pieces, axis=0)


def local_kernel(span, after, lag, first_level, pos_ref, q_ref, k_ref, v_ref, w_ref, local_ref, *refs):
    refs = list(refs)
    heads = w_ref.shape[0]
    depth_count = (k_ref.shape[0] // CHUNK).bit_length() - 1
    base_level = CHUNK.bit_length()
    received_ref = refs.pop(0) if first_level is not None else None
    copies = []
    if after is not None:
        q_hbm, w_hbm, out_ref, q_next, w_next, sems = refs
        copies = weight_copies(after, q_hbm, w_hbm, q_next, w_next, sems)
        for copy in copies:
            copy.start()
    else:
        (out_ref,) = refs
    present = (pos_ref[0] & 1) == 1

    def scores(c, h):
        start = (c - span[0]) * CHUNK
        depths = [d for d in range(depth_count) if c >> d & 1]
        stream = [k_ref[rows_of(c), columns_of(h)]]
        stream += [local_ref[h, bucket_slot(depth_count, d, c)] for d in depths]
        levels = [base_level + d for d in depths]
        if received_ref is not None:
            state = received_ref[h]
            stream.append(jnp.where(present, state, jnp.zeros_like(state)))
            levels.append(first_level)
        result = dot(
            jnp.concatenate(stream, axis=0), q_ref[rows_of(c - span[0]), columns_of(h)], TT
        )
        upper = (result[:HALF, :HALF] * local_factors(w_ref, h, start)).astype(BF16)
        lower = (result[HALF:CHUNK, HALF:] * local_factors(w_ref, h, start + HALF)).astype(BF16)
        middle_row = w_ref[h, 8:9, start + HALF : start + CHUNK] * SCALING
        middle = (result[:HALF, HALF:] * middle_row).astype(BF16)
        weighted = jnp.concatenate(
            [
                jnp.concatenate([upper, middle], axis=1),
                jnp.concatenate([jnp.zeros_like(upper), lower], axis=1),
            ],
            axis=0,
        )
        total = None
        for i, level in enumerate(levels):
            piece = result[CHUNK + i * VALUE_DIM : CHUNK + (i + 1) * VALUE_DIM]
            piece = piece * (w_ref[h, level : level + 1, start : start + CHUNK] * SCALING)
            total = piece if total is None else total + piece
        return weighted, total

    def values(c, h, weighted, total):
        inside = dot(v_ref[rows_of(c), columns_of(h)], weighted, LT)
        if total is not None:
            inside += total
        out_ref[c - span[0], columns_of(h), :] = inside.astype(BF16)

    waiting = []
    for c in range(*span):
        for h in range(heads):
            waiting.append((c, h, *scores(c, h)))
            if len(waiting) > lag:
                values(*waiting.pop(0))
    for entry in waiting:
        values(*entry)
    for copy in copies:
        copy.wait()


def across_kernel(mine, bits, first_level, spans, part, pos_ref, *refs):
    refs = list(refs)
    q_refs = [refs.pop(0) for _ in spans]
    w_refs = [refs.pop(0) for _ in spans]
    in_refs = [refs.pop(0) for _ in spans]
    state_refs = [refs.pop(0) for _ in range(bits)]
    mix_ref, square_ref = refs[-2:]
    half = w_refs[0].shape[0] // 2
    position = pos_ref[0]
    own = (position & 1) * half
    first = own if mine else half - own
    squares = {}
    for i in range(half):
        head = first + i
        states = []
        for b in range(bits):
            state = state_refs[b][head if b == 0 else i]
            states.append(jnp.where((position >> b & 1) == 1, state, jnp.zeros_like(state)))
        for c in range(*part):
            s = [low <= c < high for low, high in spans].index(True)
            local = c - spans[s][0]
            start = local * CHUNK
            used = range(0 if s == 0 else 1, bits)
            total = in_refs[s][local, columns_of(head), :].astype(jnp.float32)
            if len(used):
                stream = jnp.concatenate([states[b] for b in used], axis=0)
                result = dot(stream, q_refs[s][rows_of(local), columns_of(head)], TT)
                for n, b in enumerate(used):
                    level = first_level + b
                    row = w_refs[s][head, level : level + 1, start : start + CHUNK] * SCALING
                    total += result[n * VALUE_DIM : (n + 1) * VALUE_DIM] * row
            square = jnp.sum((total * total).reshape(VALUE_DIM // GROUP, GROUP, CHUNK), axis=0)
            squares[c] = squares[c] + square if c in squares else square
            mix_ref[rows_of(c - part[0]), columns_of(i)] = total.astype(BF16).T
    for c in range(*part):
        here = rows_of(c - part[0])
        square = jnp.sum(squares[c], axis=0, keepdims=True)
        if not mine:
            square += refs[0][:, rows_of(c)]
        square_ref[:, here] = square


def norm_kernel(width, step, low, pos_ref, own_ref, other_ref, gain_ref, square_ref, *refs):
    out_ref = refs[-1]
    i = pl.program_id(0)
    half = own_ref.shape[1]
    own = (pos_ref[0] & 1) * half
    factor = lax.rsqrt(square_ref[...] / width + 1e-05)
    column = jnp.broadcast_to(factor, (GROUP, step)).T[:, :1]
    for mix_ref, at, first in ((own_ref, low + i, own), (other_ref, i, half - own)):
        here = pl.ds(pl.multiple_of(at * step, step), step)
        there = pl.ds(pl.multiple_of(first, HEAD_DIM), half)
        mixture = mix_ref[here, :].astype(jnp.float32)
        out_ref[:, there] = (mixture * gain_ref[:, there] * column).astype(out_ref.dtype)


def body(queries, key_vectors, value_vectors, level_weights, norm_gain):
    rows, columns = queries.shape
    heads = level_weights.shape[0]
    levels = level_weights.shape[1]
    half = heads // 2
    chunks = rows // CHUNK
    depth_count = chunks.bit_length() - 1
    first_level = rows.bit_length()
    seq_size = lax.axis_size("seq")
    head_size = lax.axis_size("head")
    cross_bits = seq_size.bit_length() - 1
    position = lax.axis_index("seq").astype(jnp.int32).reshape(1)
    scalar = pl.BlockSpec(memory_space=pltpu.SMEM)

    def call(kernel, name, operands, out_shape, flops=0, size=0, limit=8, in_specs=None, **settings):
        if in_specs is None:
            in_specs = [scalar] + [WHOLE] * (len(operands) - 1)
        if "out_specs" not in settings:
            settings["out_specs"] = jax.tree.map(lambda _: WHOLE, out_shape)
        return pl.pallas_call(
            kernel,
            name=name,
            in_specs=in_specs,
            out_shape=out_shape,
            compiler_params=pltpu.CompilerParams(vmem_limit_bytes=limit * MIB),
            cost_estimate=pl.CostEstimate(
                flops=int(flops), bytes_accessed=int(size), transcendentals=0
            ),
            **settings,
        )(*operands)

    cuts = sorted({0, chunks // 4, chunks * 7 // 8, chunks})
    spans = list(zip(cuts[:-1], cuts[1:]))

    def weight_shapes(span):
        count = (span[1] - span[0]) * CHUNK
        return [
            pltpu.VMEM((count, columns), BF16),
            pltpu.VMEM((heads, levels, count), jnp.float32),
        ]

    per_chunk = 2 * heads * CHUNK * 128 * 128
    queries, level_weights = leave(queries), leave(level_weights)
    keys, values, local_states, block_state, query, weight = call(
        functools.partial(state_kernel, spans[0]),
        "states",
        [position, leave(key_vectors), leave(value_vectors), queries, level_weights],
        [
            pltpu.VMEM((rows, columns), BF16),
            pltpu.VMEM((rows, columns), BF16),
            pltpu.VMEM((heads, chunks - 1, VALUE_DIM, HEAD_DIM), BF16),
            jax.ShapeDtypeStruct((heads, VALUE_DIM, HEAD_DIM), BF16),
        ]
        + weight_shapes(spans[0]),
        flops=chunks * per_chunk,
        size=4 * rows * columns,
        in_specs=[scalar] + [ANYWHERE] * 4,
        scratch_shapes=[
            pltpu.VMEM((depth_count, heads, VALUE_DIM, HEAD_DIM), jnp.float32),
            pltpu.SemaphoreType.DMA((2, chunks)),
            pltpu.SemaphoreType.DMA((2,)),
        ],
    )
    keys, values, local_states = keep(keys), keep(values), keep(local_states)

    def swap(array, bit):
        return lax.ppermute(array, "seq", [(i, i ^ (1 << bit)) for i in range(seq_size)])

    def add(mine, received, whole):
        return call(
            functools.partial(sum_kernel, whole),
            "sum",
            [position, mine, received],
            jax.ShapeDtypeStruct((half, VALUE_DIM, HEAD_DIM), BF16),
            limit=4,
        )

    received = swap(block_state, 0)
    own_buckets, other_buckets = [received], [received]
    running = add(block_state, received, True)
    for b in range(1, cross_bits):
        received = swap(running, b)
        own_buckets.append(received)
        other_buckets.append(swap(received, 0))
        if b + 1 < cross_bits:
            running = add(running, received, False)

    insides, query_parts, weight_parts = [], [], []
    for p, span in enumerate(spans):
        count = span[1] - span[0]
        after = spans[p + 1] if p + 1 < len(spans) else None
        query, weight = keep(query), keep(weight)
        query_parts.append(query)
        weight_parts.append(weight)
        operands = [position, query, keys, values, weight, local_states]
        if p > 0:
            operands.append(own_buckets[0])
        in_specs = [scalar] + [WHOLE] * (len(operands) - 1)
        out_shape = [pltpu.VMEM((count, columns, CHUNK), BF16)]
        scratch = []
        if after is not None:
            operands += [queries, level_weights]
            in_specs += [ANYWHERE] * 2
            out_shape += weight_shapes(after)
            scratch = [pltpu.SemaphoreType.DMA((2,))]
        results = call(
            functools.partial(local_kernel, span, after, 2, first_level if p else None),
            "local",
            operands,
            out_shape,
            flops=count * per_chunk * 18,
            in_specs=in_specs,
            scratch_shapes=scratch,
        )
        insides.append(keep(results[0]))
        if after is not None:
            query, weight = results[1:]

    shared = [position, *query_parts, *weight_parts, *insides]
    own_mix, own_square = call(
        functools.partial(across_kernel, True, cross_bits, first_level, spans, (0, chunks)),
        "across",
        shared + own_buckets,
        [
            pltpu.VMEM((rows, columns // 2), BF16),
            jax.ShapeDtypeStruct((1, rows), jnp.float32),
        ],
        flops=chunks * per_chunk * 6,
    )
    parts = [(0, chunks // 2), (chunks // 2, chunks)]
    mixes, squares = [], []
    for part in parts:
        count = part[1] - part[0]
        mix, square = call(
            functools.partial(across_kernel, False, cross_bits, first_level, spans, part),
            "across",
            shared + other_buckets + [own_square],
            [
                pltpu.VMEM((count * CHUNK, columns // 2), BF16),
                jax.ShapeDtypeStruct((1, count * CHUNK), jnp.float32),
            ],
            flops=count * per_chunk * 6,
        )
        mixes.append(mix)
        bit = 1
        while bit < head_size:
            square = square + lax.ppermute(
                square, "head", [(i, i ^ bit) for i in range(head_size)]
            )
            bit *= 2
        squares.append(square)

    out = None
    step = CHUNK
    width = HEADS * VALUE_DIM
    for part, mix, square in zip(parts, mixes, squares):
        steps = part[1] - part[0]
        operands = [position, keep(own_mix), keep(mix), norm_gain.reshape(1, -1), square]
        in_specs = [
            scalar,
            WHOLE,
            WHOLE,
            pl.BlockSpec((1, columns), lambda i: (0, 0)),
            pl.BlockSpec((1, step), lambda i: (0, i)),
        ]
        aliases = {}
        if out is not None:
            operands.append(out)
            in_specs.append(ANYWHERE)
            aliases = {5: 0}
        out = call(
            functools.partial(norm_kernel, width, step, part[0]),
            "norm",
            operands,
            jax.ShapeDtypeStruct((rows, columns), BF16),
            flops=3 * rows * columns,
            size=2 * steps * step * columns,
            in_specs=in_specs,
            out_specs=pl.BlockSpec((step, columns), lambda i, low=part[0]: (i + low, 0)),
            grid=(steps,),
            input_output_aliases=aliases,
        )
    return out


def solution(mesh):
    placed = (
        P("seq", "head"),
        P("seq", "head"),
        P("seq", "head"),
        P("head", None, "seq"),
        P("head"),
    )
    return jax.shard_map(
        body, mesh=mesh, in_specs=placed, out_specs=P("seq", "head"), check_vma=False
    )
```

```python
import functools

import jax
import jax.numpy as jnp
from jax import lax
from jax.experimental import pallas as pl
from jax.experimental.pallas import tpu as pltpu
from jax.sharding import PartitionSpec as P

HEADS = 64
HEAD_DIM = 128
VALUE_DIM = 128
CHUNK = 256
HALF = 128
GROUP = 8
SCALING = HEAD_DIM ** (-0.5)
MIB = 1 << 20
BF16 = jnp.bfloat16

TT = (((1,), (1,)), ((), ()))
LT = (((0,), (0,)), ((), ()))

WHOLE = pl.BlockSpec(memory_space=pltpu.VMEM)
ANYWHERE = pl.BlockSpec(memory_space=pl.ANY)


def dot(a, b, dims):
    return lax.dot_general(a, b, dims, preferred_element_type=jnp.float32)


def keep(array):
    return pltpu.with_memory_space_constraint(array, pltpu.VMEM)


def leave(array):
    return pltpu.with_memory_space_constraint(array, pltpu.HBM)


def columns_of(head):
    if isinstance(head, int):
        return slice(head * HEAD_DIM, (head + 1) * HEAD_DIM)
    return pl.ds(pl.multiple_of(head * HEAD_DIM, HEAD_DIM), HEAD_DIM)


def rows_of(chunk):
    return slice(chunk * CHUNK, (chunk + 1) * CHUNK)


def bucket_slot(depth_count, depth, chunk):
    before = sum(1 << (depth_count - d - 1) for d in range(depth))
    return before + (((chunk >> depth) - 1) >> 1)


def state_kernel(
    span, pos_ref, k_hbm, v_hbm, q_hbm, w_hbm,
    k_ref, v_ref, local_ref, block_ref, q_ref, w_ref, held, sems, more_sems,
):
    del pos_ref
    rows = k_ref.shape[0]
    heads = block_ref.shape[0]
    chunks = rows // CHUNK
    depth_count = chunks.bit_length() - 1
    copies = []
    for c in range(chunks):
        here = pl.ds(c * CHUNK, CHUNK)
        pair = [
            pltpu.make_async_copy(k_hbm.at[here], k_ref.at[here], sems.at[0, c]),
            pltpu.make_async_copy(v_hbm.at[here], v_ref.at[here], sems.at[1, c]),
        ]
        for copy in pair:
            copy.start()
        copies.append(pair)
    more = [
        pltpu.make_async_copy(w_hbm, w_ref, more_sems.at[0]),
        query_copy(span, q_hbm, q_ref, more_sems.at[1]),
    ]
    for c in range(chunks):
        for copy in copies[c]:
            copy.wait()
        if c == chunks // 2:
            for copy in more:
                copy.start()
        for h in range(heads):
            state = dot(v_ref[rows_of(c), columns_of(h)], k_ref[rows_of(c), columns_of(h)], LT)
            depth = 0
            while c >> depth & 1:
                state += held[depth, h]
                depth += 1
            if depth < depth_count:
                held[depth, h] = state
                slot = bucket_slot(depth_count, depth, c | (1 << depth))
                local_ref[h, slot] = state.astype(BF16)
            else:
                block_ref[h] = state.astype(BF16)
    for copy in more:
        copy.wait()


def query_copy(span, q_hbm, q_ref, sem):
    here = pl.ds(span[0] * CHUNK, (span[1] - span[0]) * CHUNK)
    return pltpu.make_async_copy(q_hbm.at[here], q_ref, sem)


def sum_kernel(whole, pos_ref, mine_ref, received_ref, after_ref, out_ref):
    del after_ref
    half = out_ref.shape[0]
    here = pl.ds((pos_ref[0] & 1) * half if whole else 0, half)
    total = mine_ref[here].astype(jnp.float32) + received_ref[here].astype(jnp.float32)
    out_ref[...] = total.astype(BF16)


def local_factors(w_ref, head, start):
    def row(level):
        return w_ref[head, level : level + 1, start : start + HALF] * SCALING

    groups = HALF // GROUP
    group_id = lax.broadcasted_iota(jnp.int32, (groups, HALF), 0)
    lane_group = lax.broadcasted_iota(jnp.int32, (groups, HALF), 1) >> 3
    apart = group_id ^ lane_group
    coarse = jnp.broadcast_to(row(4), (groups, HALF))
    for level in range(5, 8):
        coarse = jnp.where(apart >= 1 << (level - 4), row(level), coarse)
    coarse = jnp.where(lane_group > group_id, coarse, 0.0)
    sub = lax.broadcasted_iota(jnp.int32, (GROUP, HALF), 0)
    lane = lax.broadcasted_iota(jnp.int32, (GROUP, HALF), 1)
    low = sub ^ (lane & 7)
    fine = jnp.broadcast_to(row(0), (GROUP, HALF))
    for level in range(1, 4):
        fine = jnp.where(low >= 1 << (level - 1), row(level), fine)
    fine = jnp.where(sub <= (lane & 7), fine, 0.0)
    pieces = []
    for g in range(groups):
        wide = jnp.broadcast_to(coarse[g : g + 1, :], (GROUP, HALF))
        pieces.append(jnp.where(lane >> 3 == g, fine, wide))
    return jnp.concatenate(pieces, axis=0)


def local_kernel(span, after, lag, first_level, pos_ref, q_ref, k_ref, v_ref, w_ref, local_ref, *refs):
    refs = list(refs)
    heads = w_ref.shape[0]
    depth_count = (k_ref.shape[0] // CHUNK).bit_length() - 1
    base_level = CHUNK.bit_length()
    received_ref = refs.pop(0) if first_level is not None else None
    copies = []
    if after is not None:
        q_hbm, out_ref, q_next, sem = refs
        copies = [query_copy(after, q_hbm, q_next, sem)]
        copies[0].start()
    else:
        (out_ref,) = refs
    present = (pos_ref[0] & 1) == 1

    def scores(c, h):
        start = c * CHUNK
        depths = [d for d in range(depth_count) if c >> d & 1]
        stream = [k_ref[rows_of(c), columns_of(h)]]
        stream += [local_ref[h, bucket_slot(depth_count, d, c)] for d in depths]
        levels = [base_level + d for d in depths]
        if received_ref is not None:
            state = received_ref[h]
            stream.append(jnp.where(present, state, jnp.zeros_like(state)))
            levels.append(first_level)
        result = dot(
            jnp.concatenate(stream, axis=0), q_ref[rows_of(c - span[0]), columns_of(h)], TT
        )
        upper = (result[:HALF, :HALF] * local_factors(w_ref, h, start)).astype(BF16)
        lower = (result[HALF:CHUNK, HALF:] * local_factors(w_ref, h, start + HALF)).astype(BF16)
        middle_row = w_ref[h, 8:9, start + HALF : start + CHUNK] * SCALING
        middle = (result[:HALF, HALF:] * middle_row).astype(BF16)
        weighted = jnp.concatenate(
            [
                jnp.concatenate([upper, middle], axis=1),
                jnp.concatenate([jnp.zeros_like(upper), lower], axis=1),
            ],
            axis=0,
        )
        total = None
        for i, level in enumerate(levels):
            piece = result[CHUNK + i * VALUE_DIM : CHUNK + (i + 1) * VALUE_DIM]
            piece = piece * (w_ref[h, level : level + 1, start : start + CHUNK] * SCALING)
            total = piece if total is None else total + piece
        return weighted, total

    def values(c, h, weighted, total):
        inside = dot(v_ref[rows_of(c), columns_of(h)], weighted, LT)
        if total is not None:
            inside += total
        out_ref[c - span[0], columns_of(h), :] = inside.astype(BF16)

    waiting = []
    for c in range(*span):
        for h in range(heads):
            waiting.append((c, h, *scores(c, h)))
            if len(waiting) > lag:
                values(*waiting.pop(0))
    for entry in waiting:
        values(*entry)
    for copy in copies:
        copy.wait()


def across_kernel(mine, bits, first_level, spans, part, pos_ref, *refs):
    refs = list(refs)
    q_refs = [refs.pop(0) for _ in spans]
    w_ref = refs.pop(0)
    in_refs = [refs.pop(0) for _ in spans]
    state_refs = [refs.pop(0) for _ in range(bits)]
    mix_ref, square_ref = refs[-2:]
    half = w_ref.shape[0] // 2
    position = pos_ref[0]
    own = (position & 1) * half
    first = own if mine else half - own
    squares = {}
    for i in range(half):
        head = first + i
        states = []
        for b in range(bits):
            state = state_refs[b][head if b == 0 else i]
            states.append(jnp.where((position >> b & 1) == 1, state, jnp.zeros_like(state)))
        for c in range(*part):
            s = [low <= c < high for low, high in spans].index(True)
            local = c - spans[s][0]
            start = c * CHUNK
            used = range(0 if s == 0 else 1, bits)
            total = in_refs[s][local, columns_of(head), :].astype(jnp.float32)
            if len(used):
                stream = jnp.concatenate([states[b] for b in used], axis=0)
                result = dot(stream, q_refs[s][rows_of(local), columns_of(head)], TT)
                for n, b in enumerate(used):
                    level = first_level + b
                    row = w_ref[head, level : level + 1, start : start + CHUNK] * SCALING
                    total += result[n * VALUE_DIM : (n + 1) * VALUE_DIM] * row
            square = jnp.sum((total * total).reshape(VALUE_DIM // GROUP, GROUP, CHUNK), axis=0)
            squares[c] = squares[c] + square if c in squares else square
            mix_ref[rows_of(c - part[0]), columns_of(i)] = total.astype(BF16).T
    for c in range(*part):
        here = rows_of(c - part[0])
        square = jnp.sum(squares[c], axis=0, keepdims=True)
        if not mine:
            square += refs[0][:, rows_of(c)]
        square_ref[:, here] = square


def norm_kernel(
    width, pos_ref, own_ref, other_ref, gain_ref, square_ref, received_ref, out_hbm, out_ref, sems
):
    rows, half = own_ref.shape
    own = (pos_ref[0] & 1) * half
    step = CHUNK // 2
    slots = out_ref.shape[0] // step
    copies = []
    for i in range(rows // step):
        here = pl.ds(i * step, step)
        slot = pl.ds(i % slots * step, step)
        if i >= slots:
            copies[i - slots].wait()
        square = square_ref[:, here] + received_ref[:, here]
        factor = lax.rsqrt(square / width + 1e-05)
        column = jnp.broadcast_to(factor, (GROUP, step)).T[:, :1]
        for mix_ref, first in ((own_ref, own), (other_ref, half - own)):
            there = pl.ds(pl.multiple_of(first, HEAD_DIM), half)
            mixture = mix_ref[here, :].astype(jnp.float32)
            out_ref[slot, there] = (mixture * gain_ref[:, there] * column).astype(out_ref.dtype)
        copy = pltpu.make_async_copy(out_ref.at[slot], out_hbm.at[here], sems.at[i])
        copy.start()
        copies.append(copy)
    for copy in copies[-slots:]:
        copy.wait()


def body(queries, key_vectors, value_vectors, level_weights, norm_gain):
    rows, columns = queries.shape
    heads = level_weights.shape[0]
    levels = level_weights.shape[1]
    half = heads // 2
    chunks = rows // CHUNK
    depth_count = chunks.bit_length() - 1
    first_level = rows.bit_length()
    seq_size = lax.axis_size("seq")
    head_size = lax.axis_size("head")
    cross_bits = seq_size.bit_length() - 1
    position = lax.axis_index("seq").astype(jnp.int32).reshape(1)
    scalar = pl.BlockSpec(memory_space=pltpu.SMEM)

    def call(kernel, name, operands, out_shape, flops=0, size=0, limit=8, in_specs=None, **settings):
        if in_specs is None:
            in_specs = [scalar] + [WHOLE] * (len(operands) - 1)
        if "out_specs" not in settings:
            settings["out_specs"] = jax.tree.map(lambda _: WHOLE, out_shape)
        return pl.pallas_call(
            kernel,
            name=name,
            in_specs=in_specs,
            out_shape=out_shape,
            compiler_params=pltpu.CompilerParams(vmem_limit_bytes=limit * MIB),
            cost_estimate=pl.CostEstimate(
                flops=int(flops), bytes_accessed=int(size), transcendentals=0
            ),
            **settings,
        )(*operands)

    cuts = sorted({0, chunks // 8, chunks * 5 // 8, chunks})
    spans = list(zip(cuts[:-1], cuts[1:]))

    def query_shape(span):
        return pltpu.VMEM(((span[1] - span[0]) * CHUNK, columns), BF16)

    per_chunk = 2 * heads * CHUNK * 128 * 128
    queries, level_weights = leave(queries), leave(level_weights)
    keys, values, local_states, block_state, query, weight = call(
        functools.partial(state_kernel, spans[0]),
        "states",
        [position, leave(key_vectors), leave(value_vectors), queries, level_weights],
        [
            pltpu.VMEM((rows, columns), BF16),
            pltpu.VMEM((rows, columns), BF16),
            pltpu.VMEM((heads, chunks - 1, VALUE_DIM, HEAD_DIM), BF16),
            jax.ShapeDtypeStruct((heads, VALUE_DIM, HEAD_DIM), BF16),
        ]
        + [query_shape(spans[0]), pltpu.VMEM((heads, levels, rows), jnp.float32)],
        flops=chunks * per_chunk,
        size=4 * rows * columns,
        in_specs=[scalar] + [ANYWHERE] * 4,
        scratch_shapes=[
            pltpu.VMEM((depth_count, heads, VALUE_DIM, HEAD_DIM), jnp.float32),
            pltpu.SemaphoreType.DMA((2, chunks)),
            pltpu.SemaphoreType.DMA((2,)),
        ],
    )
    weight = keep(weight)
    keys, values, local_states = keep(keys), keep(values), keep(local_states)

    def swap(array, bit):
        return lax.ppermute(array, "seq", [(i, i ^ (1 << bit)) for i in range(seq_size)])

    def add(mine, received, after, whole):
        return call(
            functools.partial(sum_kernel, whole),
            "sum",
            [position, mine, received, after],
            jax.ShapeDtypeStruct((half, VALUE_DIM, HEAD_DIM), BF16),
            limit=4,
            in_specs=[scalar, WHOLE, WHOLE, WHOLE],
        )

    received = swap(block_state, 0)
    own_buckets, other_buckets = [received], [received]
    running = block_state
    insides, query_parts = [], []
    for p, span in enumerate(spans):
        count = span[1] - span[0]
        after = spans[p + 1] if p + 1 < len(spans) else None
        query = keep(query)
        query_parts.append(query)
        operands = [position, query, keys, values, weight, local_states]
        if p > 0:
            operands.append(own_buckets[0])
        in_specs = [scalar] + [WHOLE] * (len(operands) - 1)
        out_shape = [pltpu.VMEM((count, columns, CHUNK), BF16)]
        scratch = []
        if after is not None:
            operands.append(queries)
            in_specs.append(ANYWHERE)
            out_shape.append(query_shape(after))
            scratch = [pltpu.SemaphoreType.DMA(())]
        results = call(
            functools.partial(local_kernel, span, after, 2, first_level if p else None),
            "local",
            operands,
            out_shape,
            flops=count * per_chunk * 18,
            in_specs=in_specs,
            scratch_shapes=scratch,
        )
        insides.append(keep(results[0]))
        if after is not None:
            query = results[1]
        if p + 1 < cross_bits:
            running = add(running, received, insides[-1], p == 0)
            received = swap(running, p + 1)
            own_buckets.append(received)
            other_buckets.append(swap(received, 0))
    for b in range(len(spans) + 1, cross_bits):
        running = add(running, received, insides[-1], False)
        received = swap(running, b)
        own_buckets.append(received)
        other_buckets.append(swap(received, 0))

    shared = [position, *query_parts, weight, *insides]

    def across(mine, operands):
        return call(
            functools.partial(across_kernel, mine, cross_bits, first_level, spans, (0, chunks)),
            "across",
            operands,
            [
                pltpu.VMEM((rows, columns // 2), BF16),
                jax.ShapeDtypeStruct((1, rows), jnp.float32),
            ],
            flops=chunks * per_chunk * 6,
        )

    own_mix, square = across(True, shared + own_buckets)
    other_mix, square = across(False, shared + other_buckets + [square])
    received = jnp.zeros_like(square)
    bit = 1
    while bit < head_size:
        if bit > 1:
            square = square + received
        received = lax.ppermute(square, "head", [(i, i ^ bit) for i in range(head_size)])
        bit *= 2
    return call(
        functools.partial(norm_kernel, HEADS * VALUE_DIM),
        "norm",
        [position, keep(own_mix), keep(other_mix), norm_gain.reshape(1, -1), square, received],
        jax.ShapeDtypeStruct((rows, columns), BF16),
        flops=3 * rows * columns,
        size=2 * rows * columns,
        out_specs=ANYWHERE,
        scratch_shapes=[
            pltpu.VMEM((rows // 2, columns), BF16),
            pltpu.SemaphoreType.DMA((2 * chunks,)),
        ],
    )


def solution(mesh):
    placed = (
        P("seq", "head"),
        P("seq", "head"),
        P("seq", "head"),
        P("head", None, "seq"),
        P("head"),
    )
    return jax.shard_map(
        body, mesh=mesh, in_specs=placed, out_specs=P("seq", "head"), check_vma=False
    )
```

```python
import functools

import jax
import jax.numpy as jnp
from jax import lax
from jax.experimental import pallas as pl
from jax.experimental.pallas import tpu as pltpu
from jax.sharding import PartitionSpec as P

HEADS = 64
HEAD_DIM = 128
VALUE_DIM = 128
CHUNK = 256
HALF = 128
GROUP = 8
SCALING = HEAD_DIM ** (-0.5)
MIB = 1 << 20
BF16 = jnp.bfloat16

TT = (((1,), (1,)), ((), ()))
LT = (((0,), (0,)), ((), ()))

WHOLE = pl.BlockSpec(memory_space=pltpu.VMEM)
ANYWHERE = pl.BlockSpec(memory_space=pl.ANY)


def dot(a, b, dims):
    return lax.dot_general(a, b, dims, preferred_element_type=jnp.float32)


def keep(array):
    return pltpu.with_memory_space_constraint(array, pltpu.VMEM)


def leave(array):
    return pltpu.with_memory_space_constraint(array, pltpu.HBM)


def columns_of(head):
    if isinstance(head, int):
        return slice(head * HEAD_DIM, (head + 1) * HEAD_DIM)
    return pl.ds(pl.multiple_of(head * HEAD_DIM, HEAD_DIM), HEAD_DIM)


def rows_of(chunk):
    return slice(chunk * CHUNK, (chunk + 1) * CHUNK)


def bucket_slot(depth_count, depth, chunk):
    before = sum(1 << (depth_count - d - 1) for d in range(depth))
    return before + (((chunk >> depth) - 1) >> 1)


def state_kernel(
    span, pos_ref, k_hbm, v_hbm, q_hbm, w_hbm,
    k_ref, v_ref, local_ref, block_ref, q_ref, w_ref, held, sems, more_sems,
):
    del pos_ref
    rows = k_ref.shape[0]
    heads = block_ref.shape[0]
    chunks = rows // CHUNK
    depth_count = chunks.bit_length() - 1
    copies = []
    for c in range(chunks):
        here = pl.ds(c * CHUNK, CHUNK)
        pair = [
            pltpu.make_async_copy(k_hbm.at[here], k_ref.at[here], sems.at[0, c]),
            pltpu.make_async_copy(v_hbm.at[here], v_ref.at[here], sems.at[1, c]),
        ]
        for copy in pair:
            copy.start()
        copies.append(pair)
    more = [
        pltpu.make_async_copy(w_hbm, w_ref, more_sems.at[0]),
        query_copy(span, q_hbm, q_ref, more_sems.at[1]),
    ]
    for c in range(chunks):
        for copy in copies[c]:
            copy.wait()
        if c == chunks // 2:
            for copy in more:
                copy.start()
        for h in range(heads):
            state = dot(v_ref[rows_of(c), columns_of(h)], k_ref[rows_of(c), columns_of(h)], LT)
            depth = 0
            while c >> depth & 1:
                state += held[depth, h]
                depth += 1
            if depth < depth_count:
                held[depth, h] = state
                slot = bucket_slot(depth_count, depth, c | (1 << depth))
                local_ref[h, slot] = state.astype(BF16)
            else:
                block_ref[h] = state.astype(BF16)
    for copy in more:
        copy.wait()


def query_copy(span, q_hbm, q_ref, sem):
    here = pl.ds(span[0] * CHUNK, (span[1] - span[0]) * CHUNK)
    return pltpu.make_async_copy(q_hbm.at[here], q_ref, sem)


def sum_kernel(whole, pos_ref, mine_ref, received_ref, after_ref, out_ref):
    del after_ref
    half = out_ref.shape[0]
    here = pl.ds((pos_ref[0] & 1) * half if whole else 0, half)
    total = mine_ref[here].astype(jnp.float32) + received_ref[here].astype(jnp.float32)
    out_ref[...] = total.astype(BF16)


def stack_kernel(*refs):
    out_ref = refs[-1]
    for b, ref in enumerate(refs[:-1]):
        out_ref[b] = ref[...]


def local_factors(w_ref, head, start):
    def row(level):
        return w_ref[head, level : level + 1, start : start + HALF] * SCALING

    groups = HALF // GROUP
    group_id = lax.broadcasted_iota(jnp.int32, (groups, HALF), 0)
    lane_group = lax.broadcasted_iota(jnp.int32, (groups, HALF), 1) >> 3
    apart = group_id ^ lane_group
    coarse = jnp.broadcast_to(row(4), (groups, HALF))
    for level in range(5, 8):
        coarse = jnp.where(apart >= 1 << (level - 4), row(level), coarse)
    coarse = jnp.where(lane_group > group_id, coarse, 0.0)
    sub = lax.broadcasted_iota(jnp.int32, (GROUP, HALF), 0)
    lane = lax.broadcasted_iota(jnp.int32, (GROUP, HALF), 1)
    low = sub ^ (lane & 7)
    fine = jnp.broadcast_to(row(0), (GROUP, HALF))
    for level in range(1, 4):
        fine = jnp.where(low >= 1 << (level - 1), row(level), fine)
    fine = jnp.where(sub <= (lane & 7), fine, 0.0)
    pieces = []
    for g in range(groups):
        wide = jnp.broadcast_to(coarse[g : g + 1, :], (GROUP, HALF))
        pieces.append(jnp.where(lane >> 3 == g, fine, wide))
    return jnp.concatenate(pieces, axis=0)


def local_kernel(span, after, lag, first_level, pos_ref, q_ref, k_ref, v_ref, w_ref, local_ref, *refs):
    refs = list(refs)
    heads = w_ref.shape[0]
    depth_count = (k_ref.shape[0] // CHUNK).bit_length() - 1
    base_level = CHUNK.bit_length()
    received_ref = refs.pop(0) if first_level is not None else None
    copies = []
    if after is not None:
        q_hbm, out_ref, q_next, sem = refs
        copies = [query_copy(after, q_hbm, q_next, sem)]
        copies[0].start()
    else:
        (out_ref,) = refs
    present = (pos_ref[0] & 1) == 1

    def scores(c, h):
        start = c * CHUNK
        depths = [d for d in range(depth_count) if c >> d & 1]
        stream = [k_ref[rows_of(c), columns_of(h)]]
        stream += [local_ref[h, bucket_slot(depth_count, d, c)] for d in depths]
        levels = [base_level + d for d in depths]
        if received_ref is not None:
            state = received_ref[h]
            stream.append(jnp.where(present, state, jnp.zeros_like(state)))
            levels.append(first_level)
        result = dot(
            jnp.concatenate(stream, axis=0), q_ref[rows_of(c - span[0]), columns_of(h)], TT
        )
        upper = (result[:HALF, :HALF] * local_factors(w_ref, h, start)).astype(BF16)
        lower = (result[HALF:CHUNK, HALF:] * local_factors(w_ref, h, start + HALF)).astype(BF16)
        middle_row = w_ref[h, 8:9, start + HALF : start + CHUNK] * SCALING
        middle = (result[:HALF, HALF:] * middle_row).astype(BF16)
        weighted = jnp.concatenate(
            [
                jnp.concatenate([upper, middle], axis=1),
                jnp.concatenate([jnp.zeros_like(upper), lower], axis=1),
            ],
            axis=0,
        )
        total = None
        for i, level in enumerate(levels):
            piece = result[CHUNK + i * VALUE_DIM : CHUNK + (i + 1) * VALUE_DIM]
            piece = piece * (w_ref[h, level : level + 1, start : start + CHUNK] * SCALING)
            total = piece if total is None else total + piece
        return weighted, total

    def values(c, h, weighted, total):
        inside = dot(v_ref[rows_of(c), columns_of(h)], weighted, LT)
        if total is not None:
            inside += total
        out_ref[c - span[0], columns_of(h), :] = inside.astype(BF16)

    waiting = []
    for c in range(*span):
        for h in range(heads):
            waiting.append((c, h, *scores(c, h)))
            if len(waiting) > lag:
                values(*waiting.pop(0))
    for entry in waiting:
        values(*entry)
    for copy in copies:
        copy.wait()


def across_kernel(mine, bits, first_level, spans, part, pos_ref, *refs):
    refs = list(refs)
    q_refs = [refs.pop(0) for _ in spans]
    w_ref = refs.pop(0)
    in_refs = [refs.pop(0) for _ in spans]
    first_ref = refs.pop(0)
    rest_ref = refs.pop(0) if bits > 1 else None
    mix_ref, square_ref = refs[-2:]
    half = w_ref.shape[0] // 2
    position = pos_ref[0]
    own = (position & 1) * half
    first = own if mine else half - own
    squares = {}
    for i in range(half):
        head = first + i
        states = []
        for b in range(bits):
            state = first_ref[head] if b == 0 else rest_ref[b - 1, i]
            states.append(jnp.where((position >> b & 1) == 1, state, jnp.zeros_like(state)))
        for c in range(*part):
            s = [low <= c < high for low, high in spans].index(True)
            local = c - spans[s][0]
            start = c * CHUNK
            used = range(0 if s == 0 else 1, bits)
            total = in_refs[s][local, columns_of(head), :].astype(jnp.float32)
            if len(used):
                stream = jnp.concatenate([states[b] for b in used], axis=0)
                result = dot(stream, q_refs[s][rows_of(local), columns_of(head)], TT)
                for n, b in enumerate(used):
                    level = first_level + b
                    row = w_ref[head, level : level + 1, start : start + CHUNK] * SCALING
                    total += result[n * VALUE_DIM : (n + 1) * VALUE_DIM] * row
            square = jnp.sum((total * total).reshape(VALUE_DIM // GROUP, GROUP, CHUNK), axis=0)
            squares[c] = squares[c] + square if c in squares else square
            mix_ref[rows_of(c - part[0]), columns_of(i)] = total.astype(BF16).T
    for c in range(*part):
        here = rows_of(c - part[0])
        square = jnp.sum(squares[c], axis=0, keepdims=True)
        if not mine:
            square += refs[0][:, rows_of(c)]
        square_ref[:, here] = square


def norm_kernel(
    width, pos_ref, own_ref, other_ref, gain_ref, *refs
):
    *square_refs, out_hbm, out_ref, sems = refs
    rows, half = own_ref.shape
    own = (pos_ref[0] & 1) * half
    step = CHUNK // 2
    slots = out_ref.shape[0] // step
    copies = []
    for i in range(rows // step):
        here = pl.ds(i * step, step)
        slot = pl.ds(i % slots * step, step)
        if i >= slots:
            copies[i - slots].wait()
        square = sum(ref[:, here] for ref in square_refs)
        factor = lax.rsqrt(square / width + 1e-05)
        column = jnp.broadcast_to(factor, (GROUP, step)).T[:, :1]
        for mix_ref, first in ((own_ref, own), (other_ref, half - own)):
            there = pl.ds(pl.multiple_of(first, HEAD_DIM), half)
            mixture = mix_ref[here, :].astype(jnp.float32)
            out_ref[slot, there] = (mixture * gain_ref[:, there] * column).astype(out_ref.dtype)
        copy = pltpu.make_async_copy(out_ref.at[slot], out_hbm.at[here], sems.at[i])
        copy.start()
        copies.append(copy)
    for copy in copies[-slots:]:
        copy.wait()


def body(queries, key_vectors, value_vectors, level_weights, norm_gain):
    rows, columns = queries.shape
    heads = level_weights.shape[0]
    levels = level_weights.shape[1]
    half = heads // 2
    chunks = rows // CHUNK
    depth_count = chunks.bit_length() - 1
    first_level = rows.bit_length()
    seq_size = lax.axis_size("seq")
    head_size = lax.axis_size("head")
    cross_bits = seq_size.bit_length() - 1
    position = lax.axis_index("seq").astype(jnp.int32).reshape(1)
    scalar = pl.BlockSpec(memory_space=pltpu.SMEM)

    def call(kernel, name, operands, out_shape, flops=0, size=0, limit=8, in_specs=None, **settings):
        if in_specs is None:
            in_specs = [scalar] + [WHOLE] * (len(operands) - 1)
        if "out_specs" not in settings:
            settings["out_specs"] = jax.tree.map(lambda _: WHOLE, out_shape)
        return pl.pallas_call(
            kernel,
            name=name,
            in_specs=in_specs,
            out_shape=out_shape,
            compiler_params=pltpu.CompilerParams(vmem_limit_bytes=limit * MIB),
            cost_estimate=pl.CostEstimate(
                flops=int(flops), bytes_accessed=int(size), transcendentals=0
            ),
            **settings,
        )(*operands)

    cuts = sorted({0, chunks // 8, chunks * 5 // 8, chunks})
    spans = list(zip(cuts[:-1], cuts[1:]))

    def query_shape(span):
        return pltpu.VMEM(((span[1] - span[0]) * CHUNK, columns), BF16)

    per_chunk = 2 * heads * CHUNK * 128 * 128
    queries, level_weights = leave(queries), leave(level_weights)
    keys, values, local_states, block_state, query, weight = call(
        functools.partial(state_kernel, spans[0]),
        "states",
        [position, leave(key_vectors), leave(value_vectors), queries, level_weights],
        [
            pltpu.VMEM((rows, columns), BF16),
            pltpu.VMEM((rows, columns), BF16),
            pltpu.VMEM((heads, chunks - 1, VALUE_DIM, HEAD_DIM), BF16),
            jax.ShapeDtypeStruct((heads, VALUE_DIM, HEAD_DIM), BF16),
        ]
        + [query_shape(spans[0]), pltpu.VMEM((heads, levels, rows), jnp.float32)],
        flops=chunks * per_chunk,
        size=4 * rows * columns,
        in_specs=[scalar] + [ANYWHERE] * 4,
        scratch_shapes=[
            pltpu.VMEM((depth_count, heads, VALUE_DIM, HEAD_DIM), jnp.float32),
            pltpu.SemaphoreType.DMA((2, chunks)),
            pltpu.SemaphoreType.DMA((2,)),
        ],
    )
    weight = keep(weight)
    keys, values, local_states = keep(keys), keep(values), keep(local_states)

    def swap(array, bit):
        return lax.ppermute(array, "seq", [(i, i ^ (1 << bit)) for i in range(seq_size)])

    def add(mine, received, after, whole):
        return call(
            functools.partial(sum_kernel, whole),
            "sum",
            [position, mine, received, after],
            jax.ShapeDtypeStruct((half, VALUE_DIM, HEAD_DIM), BF16),
            limit=4,
            in_specs=[scalar, WHOLE, WHOLE, WHOLE],
        )

    received = swap(block_state, 0)
    buckets = [received]
    running = block_state
    insides, query_parts = [], []
    for p, span in enumerate(spans):
        count = span[1] - span[0]
        after = spans[p + 1] if p + 1 < len(spans) else None
        query = keep(query)
        query_parts.append(query)
        operands = [position, query, keys, values, weight, local_states]
        if p > 0:
            operands.append(buckets[0])
        in_specs = [scalar] + [WHOLE] * (len(operands) - 1)
        out_shape = [pltpu.VMEM((count, columns, CHUNK), BF16)]
        scratch = []
        if after is not None:
            operands.append(queries)
            in_specs.append(ANYWHERE)
            out_shape.append(query_shape(after))
            scratch = [pltpu.SemaphoreType.DMA(())]
        results = call(
            functools.partial(local_kernel, span, after, 2, first_level if p else None),
            "local",
            operands,
            out_shape,
            flops=count * per_chunk * 18,
            in_specs=in_specs,
            scratch_shapes=scratch,
        )
        insides.append(keep(results[0]))
        if after is not None:
            query = results[1]
        if p + 1 < cross_bits:
            running = add(running, received, insides[-1], p == 0)
            received = swap(running, p + 1)
            buckets.append(received)
    for b in range(len(spans) + 1, cross_bits):
        running = add(running, received, insides[-1], False)
        received = swap(running, b)
        buckets.append(received)
    own_buckets = other_buckets = buckets[:1]
    if cross_bits > 1:
        own = call(
            stack_kernel,
            "stack",
            buckets[1:],
            jax.ShapeDtypeStruct((cross_bits - 1, half, VALUE_DIM, HEAD_DIM), BF16),
            in_specs=[WHOLE] * (cross_bits - 1),
        )
        own_buckets = buckets[:1] + [own]
        other_buckets = buckets[:1] + [swap(own, 0)]

    shared = [position, *query_parts, weight, *insides]

    def across(mine, operands):
        return call(
            functools.partial(across_kernel, mine, cross_bits, first_level, spans, (0, chunks)),
            "across",
            operands,
            [
                pltpu.VMEM((rows, columns // 2), BF16),
                jax.ShapeDtypeStruct((1, rows), jnp.float32),
            ],
            flops=chunks * per_chunk * 6,
        )

    own_mix, square = across(True, shared + own_buckets)
    other_mix, square = across(False, shared + other_buckets + [square])
    squares = [square]
    for other in range(1, head_size):
        squares.append(
            lax.ppermute(square, "head", [(i, i ^ other) for i in range(head_size)])
        )
    return call(
        functools.partial(norm_kernel, HEADS * VALUE_DIM),
        "norm",
        [position, keep(own_mix), keep(other_mix), norm_gain.reshape(1, -1), *squares],
        jax.ShapeDtypeStruct((rows, columns), BF16),
        flops=3 * rows * columns,
        size=2 * rows * columns,
        out_specs=ANYWHERE,
        scratch_shapes=[
            pltpu.VMEM((rows // 2, columns), BF16),
            pltpu.SemaphoreType.DMA((2 * chunks,)),
        ],
    )


def solution(mesh):
    placed = (
        P("seq", "head"),
        P("seq", "head"),
        P("seq", "head"),
        P("head", None, "seq"),
        P("head"),
    )
    return jax.shard_map(
        body, mesh=mesh, in_specs=placed, out_specs=P("seq", "head"), check_vma=False
    )
```

```python
import functools

import jax
import jax.numpy as jnp
from jax import lax
from jax.experimental import pallas as pl
from jax.experimental.pallas import tpu as pltpu
from jax.sharding import PartitionSpec as P

HEADS = 64
HEAD_DIM = 128
VALUE_DIM = 128
CHUNK = 256
HALF = 128
GROUP = 8
SCALING = HEAD_DIM ** (-0.5)
MIB = 1 << 20
BF16 = jnp.bfloat16

TT = (((1,), (1,)), ((), ()))
LT = (((0,), (0,)), ((), ()))

WHOLE = pl.BlockSpec(memory_space=pltpu.VMEM)
ANYWHERE = pl.BlockSpec(memory_space=pl.ANY)


def dot(a, b, dims):
    return lax.dot_general(a, b, dims, preferred_element_type=jnp.float32)


def keep(array):
    return pltpu.with_memory_space_constraint(array, pltpu.VMEM)


def leave(array):
    return pltpu.with_memory_space_constraint(array, pltpu.HBM)


def columns_of(head):
    if isinstance(head, int):
        return slice(head * HEAD_DIM, (head + 1) * HEAD_DIM)
    return pl.ds(pl.multiple_of(head * HEAD_DIM, HEAD_DIM), HEAD_DIM)


def rows_of(chunk):
    return slice(chunk * CHUNK, (chunk + 1) * CHUNK)


def bucket_slot(depth_count, depth, chunk):
    before = sum(1 << (depth_count - d - 1) for d in range(depth))
    return before + (((chunk >> depth) - 1) >> 1)


def state_kernel(
    span, pos_ref, k_hbm, v_hbm, q_hbm, w_hbm,
    k_ref, v_ref, local_ref, block_ref, q_ref, w_ref, held, sems, more_sems,
):
    del pos_ref
    rows = k_ref.shape[0]
    heads = block_ref.shape[0]
    chunks = rows // CHUNK
    depth_count = chunks.bit_length() - 1
    copies = []
    for c in range(chunks):
        here = pl.ds(c * CHUNK, CHUNK)
        pair = [
            pltpu.make_async_copy(k_hbm.at[here], k_ref.at[here], sems.at[0, c]),
            pltpu.make_async_copy(v_hbm.at[here], v_ref.at[here], sems.at[1, c]),
        ]
        for copy in pair:
            copy.start()
        copies.append(pair)
    more = [
        pltpu.make_async_copy(w_hbm, w_ref, more_sems.at[0]),
        query_copy(span, q_hbm, q_ref, more_sems.at[1]),
    ]
    for c in range(chunks):
        for copy in copies[c]:
            copy.wait()
        if c == chunks // 2:
            for copy in more:
                copy.start()
        for h in range(heads):
            state = dot(v_ref[rows_of(c), columns_of(h)], k_ref[rows_of(c), columns_of(h)], LT)
            depth = 0
            while c >> depth & 1:
                state += held[depth, h]
                depth += 1
            if depth < depth_count:
                held[depth, h] = state
                slot = bucket_slot(depth_count, depth, c | (1 << depth))
                local_ref[h, slot] = state.astype(BF16)
            else:
                block_ref[h] = state.astype(BF16)
    for copy in more:
        copy.wait()


def query_copy(span, q_hbm, q_ref, sem):
    here = pl.ds(span[0] * CHUNK, (span[1] - span[0]) * CHUNK)
    return pltpu.make_async_copy(q_hbm.at[here], q_ref, sem)


def sum_kernel(whole, pos_ref, mine_ref, received_ref, after_ref, out_ref):
    del after_ref
    half = out_ref.shape[0]
    here = pl.ds((pos_ref[0] & 1) * half if whole else 0, half)
    total = mine_ref[here].astype(jnp.float32) + received_ref[here].astype(jnp.float32)
    out_ref[...] = total.astype(BF16)


def stack_kernel(*refs):
    out_ref = refs[-1]
    for b, ref in enumerate(refs[:-1]):
        out_ref[b] = ref[...]


def local_factors(w_ref, head, start):
    def row(level):
        return w_ref[head, level : level + 1, start : start + HALF] * SCALING

    groups = HALF // GROUP
    group_id = lax.broadcasted_iota(jnp.int32, (groups, HALF), 0)
    lane_group = lax.broadcasted_iota(jnp.int32, (groups, HALF), 1) >> 3
    apart = group_id ^ lane_group
    coarse = jnp.broadcast_to(row(4), (groups, HALF))
    for level in range(5, 8):
        coarse = jnp.where(apart >= 1 << (level - 4), row(level), coarse)
    coarse = jnp.where(lane_group > group_id, coarse, 0.0)
    sub = lax.broadcasted_iota(jnp.int32, (GROUP, HALF), 0)
    lane = lax.broadcasted_iota(jnp.int32, (GROUP, HALF), 1)
    low = sub ^ (lane & 7)
    fine = jnp.broadcast_to(row(0), (GROUP, HALF))
    for level in range(1, 4):
        fine = jnp.where(low >= 1 << (level - 1), row(level), fine)
    fine = jnp.where(sub <= (lane & 7), fine, 0.0)
    pieces = []
    for g in range(groups):
        wide = jnp.broadcast_to(coarse[g : g + 1, :], (GROUP, HALF))
        pieces.append(jnp.where(lane >> 3 == g, fine, wide))
    return jnp.concatenate(pieces, axis=0)


def local_kernel(
    span, given, loads, lag, first_level, buckets, pos_ref, k_ref, v_ref, w_ref, local_ref, *refs
):
    refs = list(refs)
    heads = w_ref.shape[0]
    half = heads // 2
    depth_count = (k_ref.shape[0] // CHUNK).bit_length() - 1
    base_level = CHUNK.bit_length()
    bucket_refs = [refs.pop(0) for _ in range(buckets)]
    q_refs = {part: refs.pop(0) for part in given}
    q_hbm = refs.pop(0) if loads else None
    out_ref = refs.pop(0)
    waits = []
    for i, part in enumerate(loads):
        q_refs[part] = refs.pop(0)
        waits.append((part, query_copy(part, q_hbm, q_refs[part], refs[-1].at[i])))
    position = pos_ref[0]
    own = (position & 1) * half

    def arrive():
        waits.pop(0)[1].wait()
        if waits:
            waits[0][1].start()

    if waits:
        waits[0][1].start()

    def scores(c, i, h):
        start = c * CHUNK
        depths = [d for d in range(depth_count) if c >> d & 1]
        stream = [k_ref[rows_of(c), columns_of(h)]]
        stream += [local_ref[h, bucket_slot(depth_count, d, c)] for d in depths]
        levels = [base_level + d for d in depths]
        for b, ref in enumerate(bucket_refs):
            if b == 0 or i < half:
                state = ref[h] if b == 0 else ref[i]
                present = (position >> b & 1) == 1
                stream.append(jnp.where(present, state, jnp.zeros_like(state)))
                levels.append(first_level + b)
        part = next(p for p in q_refs if p[0] <= c < p[1])
        query = q_refs[part][rows_of(c - part[0]), columns_of(h)]
        result = dot(jnp.concatenate(stream, axis=0), query, TT)
        upper = (result[:HALF, :HALF] * local_factors(w_ref, h, start)).astype(BF16)
        lower = (result[HALF:CHUNK, HALF:] * local_factors(w_ref, h, start + HALF)).astype(BF16)
        middle_row = w_ref[h, 8:9, start + HALF : start + CHUNK] * SCALING
        middle = (result[:HALF, HALF:] * middle_row).astype(BF16)
        weighted = jnp.concatenate(
            [
                jnp.concatenate([upper, middle], axis=1),
                jnp.concatenate([jnp.zeros_like(upper), lower], axis=1),
            ],
            axis=0,
        )
        total = None
        for n, level in enumerate(levels):
            piece = result[CHUNK + n * VALUE_DIM : CHUNK + (n + 1) * VALUE_DIM]
            piece = piece * (w_ref[h, level : level + 1, start : start + CHUNK] * SCALING)
            total = piece if total is None else total + piece
        return weighted, total

    def values(c, h, weighted, total):
        inside = dot(v_ref[rows_of(c), columns_of(h)], weighted, LT)
        if total is not None:
            inside += total
        out_ref[c - span[0], columns_of(h), :] = inside.astype(BF16)

    waiting = []
    for c in range(*span):
        while waits and waits[0][0][0] <= c:
            arrive()
        for i in range(heads):
            h = i
            if buckets > 1:
                h = own + i if i < half else i - own
            waiting.append((c, h, *scores(c, i, h)))
            if len(waiting) > lag:
                values(*waiting.pop(0))
    for entry in waiting:
        values(*entry)
    while waits:
        arrive()


def across_kernel(mine, bits, done, first_level, spans, parts, part, pos_ref, *refs):
    refs = list(refs)
    q_refs = {p: refs.pop(0) for p in parts}
    w_ref = refs.pop(0)
    in_refs = [refs.pop(0) for _ in spans]
    first_ref = refs.pop(0)
    rest_ref = refs.pop(0) if bits > 1 else None
    mix_ref, square_ref = refs[-2:]
    half = w_ref.shape[0] // 2
    position = pos_ref[0]
    own = (position & 1) * half
    first = own if mine else half - own
    squares = {}
    for i in range(half):
        head = first + i
        states = []
        for b in range(bits):
            state = first_ref[head] if b == 0 else rest_ref[b - 1, i]
            states.append(jnp.where((position >> b & 1) == 1, state, jnp.zeros_like(state)))
        for c in range(*part):
            s = [low <= c < high for low, high in spans].index(True)
            local = c - spans[s][0]
            start = c * CHUNK
            used = range(done[s] if mine else min(done[s], 1), bits)
            place = next(p for p in parts if p[0] <= c < p[1])
            total = in_refs[s][local, columns_of(head), :].astype(jnp.float32)
            if len(used):
                stream = jnp.concatenate([states[b] for b in used], axis=0)
                result = dot(stream, q_refs[place][rows_of(c - place[0]), columns_of(head)], TT)
                for n, b in enumerate(used):
                    level = first_level + b
                    row = w_ref[head, level : level + 1, start : start + CHUNK] * SCALING
                    total += result[n * VALUE_DIM : (n + 1) * VALUE_DIM] * row
            square = jnp.sum((total * total).reshape(VALUE_DIM // GROUP, GROUP, CHUNK), axis=0)
            squares[c] = squares[c] + square if c in squares else square
            mix_ref[rows_of(c - part[0]), columns_of(i)] = total.astype(BF16).T
    for c in range(*part):
        here = rows_of(c - part[0])
        square = jnp.sum(squares[c], axis=0, keepdims=True)
        if not mine:
            square += refs[0][:, rows_of(c)]
        square_ref[:, here] = square


def norm_kernel(
    width, pos_ref, own_ref, other_ref, gain_ref, *refs
):
    *square_refs, out_hbm, out_ref, sems = refs
    rows, half = own_ref.shape
    own = (pos_ref[0] & 1) * half
    step = CHUNK // 2
    slots = out_ref.shape[0] // step
    copies = []
    for i in range(rows // step):
        here = pl.ds(i * step, step)
        slot = pl.ds(i % slots * step, step)
        if i >= slots:
            copies[i - slots].wait()
        square = sum(ref[:, here] for ref in square_refs)
        factor = lax.rsqrt(square / width + 1e-05)
        column = jnp.broadcast_to(factor, (GROUP, step)).T[:, :1]
        for mix_ref, first in ((own_ref, own), (other_ref, half - own)):
            there = pl.ds(pl.multiple_of(first, HEAD_DIM), half)
            mixture = mix_ref[here, :].astype(jnp.float32)
            out_ref[slot, there] = (mixture * gain_ref[:, there] * column).astype(out_ref.dtype)
        copy = pltpu.make_async_copy(out_ref.at[slot], out_hbm.at[here], sems.at[i])
        copy.start()
        copies.append(copy)
    for copy in copies[-slots:]:
        copy.wait()


def body(queries, key_vectors, value_vectors, level_weights, norm_gain):
    rows, columns = queries.shape
    heads = level_weights.shape[0]
    levels = level_weights.shape[1]
    half = heads // 2
    chunks = rows // CHUNK
    depth_count = chunks.bit_length() - 1
    first_level = rows.bit_length()
    seq_size = lax.axis_size("seq")
    head_size = lax.axis_size("head")
    cross_bits = seq_size.bit_length() - 1
    position = lax.axis_index("seq").astype(jnp.int32).reshape(1)
    scalar = pl.BlockSpec(memory_space=pltpu.SMEM)

    def call(kernel, name, operands, out_shape, flops=0, size=0, limit=8, in_specs=None, **settings):
        if in_specs is None:
            in_specs = [scalar] + [WHOLE] * (len(operands) - 1)
        if "out_specs" not in settings:
            settings["out_specs"] = jax.tree.map(lambda _: WHOLE, out_shape)
        return pl.pallas_call(
            kernel,
            name=name,
            in_specs=in_specs,
            out_shape=out_shape,
            compiler_params=pltpu.CompilerParams(vmem_limit_bytes=limit * MIB),
            cost_estimate=pl.CostEstimate(
                flops=int(flops), bytes_accessed=int(size), transcendentals=0
            ),
            **settings,
        )(*operands)

    cuts = sorted({0, chunks // 8, chunks * 5 // 8, chunks})
    spans = list(zip(cuts[:-1], cuts[1:]))
    middle = (spans[1][0] + spans[1][1]) // 2
    parts = [spans[0], (spans[1][0], middle), (middle, spans[1][1]), spans[2]]
    plan = [(parts[:1], parts[1:2]), (parts[1:2], parts[2:]), (parts[3:], [])]
    done = [0, 1, min(2, cross_bits)]

    def query_shape(span):
        return pltpu.VMEM(((span[1] - span[0]) * CHUNK, columns), BF16)

    per_chunk = 2 * heads * CHUNK * 128 * 128
    queries, level_weights = leave(queries), leave(level_weights)
    keys, values, local_states, block_state, query, weight = call(
        functools.partial(state_kernel, spans[0]),
        "states",
        [position, leave(key_vectors), leave(value_vectors), queries, level_weights],
        [
            pltpu.VMEM((rows, columns), BF16),
            pltpu.VMEM((rows, columns), BF16),
            pltpu.VMEM((heads, chunks - 1, VALUE_DIM, HEAD_DIM), BF16),
            jax.ShapeDtypeStruct((heads, VALUE_DIM, HEAD_DIM), BF16),
        ]
        + [query_shape(spans[0]), pltpu.VMEM((heads, levels, rows), jnp.float32)],
        flops=chunks * per_chunk,
        size=4 * rows * columns,
        in_specs=[scalar] + [ANYWHERE] * 4,
        scratch_shapes=[
            pltpu.VMEM((depth_count, heads, VALUE_DIM, HEAD_DIM), jnp.float32),
            pltpu.SemaphoreType.DMA((2, chunks)),
            pltpu.SemaphoreType.DMA((2,)),
        ],
    )
    weight = keep(weight)
    keys, values, local_states = keep(keys), keep(values), keep(local_states)

    def swap(array, bit):
        return lax.ppermute(array, "seq", [(i, i ^ (1 << bit)) for i in range(seq_size)])

    def add(mine, received, after, whole):
        return call(
            functools.partial(sum_kernel, whole),
            "sum",
            [position, mine, received, after],
            jax.ShapeDtypeStruct((half, VALUE_DIM, HEAD_DIM), BF16),
            limit=4,
            in_specs=[scalar, WHOLE, WHOLE, WHOLE],
        )

    received = swap(block_state, 0)
    buckets = [received]
    running = block_state
    insides = []
    held = {parts[0]: keep(query)}
    for p, span in enumerate(spans):
        count = span[1] - span[0]
        given, loads = plan[p]
        operands = [position, keys, values, weight, local_states]
        operands += buckets[: done[p]] + [held[part] for part in given]
        in_specs = [scalar] + [WHOLE] * (len(operands) - 1)
        out_shape = [pltpu.VMEM((count, columns, CHUNK), BF16)]
        scratch = []
        if loads:
            operands.append(queries)
            in_specs.append(ANYWHERE)
            out_shape += [query_shape(part) for part in loads]
            scratch = [pltpu.SemaphoreType.DMA((len(loads),))]
        results = call(
            functools.partial(local_kernel, span, given, loads, 2, first_level, done[p]),
            "local",
            operands,
            out_shape,
            flops=count * per_chunk * 18,
            in_specs=in_specs,
            scratch_shapes=scratch,
        )
        insides.append(keep(results[0]))
        held.update((part, keep(array)) for part, array in zip(loads, results[1:]))
        if p + 1 < cross_bits:
            running = add(running, received, insides[-1], p == 0)
            received = swap(running, p + 1)
            buckets.append(received)
    for b in range(len(spans) + 1, cross_bits):
        running = add(running, received, insides[-1], False)
        received = swap(running, b)
        buckets.append(received)
    own_buckets = other_buckets = buckets[:1]
    if cross_bits > 1:
        own = call(
            stack_kernel,
            "stack",
            buckets[1:],
            jax.ShapeDtypeStruct((cross_bits - 1, half, VALUE_DIM, HEAD_DIM), BF16),
            in_specs=[WHOLE] * (cross_bits - 1),
        )
        own_buckets = buckets[:1] + [own]
        other_buckets = buckets[:1] + [swap(own, 0)]

    shared = [position, *[held[part] for part in parts], weight, *insides]

    def across(mine, operands):
        return call(
            functools.partial(
                across_kernel, mine, cross_bits, done, first_level, spans, parts, (0, chunks)
            ),
            "across",
            operands,
            [
                pltpu.VMEM((rows, columns // 2), BF16),
                jax.ShapeDtypeStruct((1, rows), jnp.float32),
            ],
            flops=chunks * per_chunk * 6,
        )

    own_mix, square = across(True, shared + own_buckets)
    other_mix, square = across(False, shared + other_buckets + [square])
    squares = [square]
    for other in range(1, head_size):
        squares.append(
            lax.ppermute(square, "head", [(i, i ^ other) for i in range(head_size)])
        )
    return call(
        functools.partial(norm_kernel, HEADS * VALUE_DIM),
        "norm",
        [position, keep(own_mix), keep(other_mix), norm_gain.reshape(1, -1), *squares],
        jax.ShapeDtypeStruct((rows, columns), BF16),
        flops=3 * rows * columns,
        size=2 * rows * columns,
        out_specs=ANYWHERE,
        scratch_shapes=[
            pltpu.VMEM((rows // 2, columns), BF16),
            pltpu.SemaphoreType.DMA((2 * chunks,)),
        ],
    )


def solution(mesh):
    placed = (
        P("seq", "head"),
        P("seq", "head"),
        P("seq", "head"),
        P("head", None, "seq"),
        P("head"),
    )
    return jax.shard_map(
        body, mesh=mesh, in_specs=placed, out_specs=P("seq", "head"), check_vma=False
    )
```

```python
import functools

import jax
import jax.numpy as jnp
from jax import lax
from jax.experimental import pallas as pl
from jax.experimental.pallas import tpu as pltpu
from jax.sharding import PartitionSpec as P

HEADS = 64
HEAD_DIM = 128
VALUE_DIM = 128
CHUNK = 256
HALF = 128
GROUP = 8
SCALING = HEAD_DIM ** (-0.5)
MIB = 1 << 20
BF16 = jnp.bfloat16

TT = (((1,), (1,)), ((), ()))
LT = (((0,), (0,)), ((), ()))

WHOLE = pl.BlockSpec(memory_space=pltpu.VMEM)
ANYWHERE = pl.BlockSpec(memory_space=pl.ANY)


def dot(a, b, dims):
    return lax.dot_general(a, b, dims, preferred_element_type=jnp.float32)


def keep(array):
    return pltpu.with_memory_space_constraint(array, pltpu.VMEM)


def leave(array):
    return pltpu.with_memory_space_constraint(array, pltpu.HBM)


def columns_of(head):
    if isinstance(head, int):
        return slice(head * HEAD_DIM, (head + 1) * HEAD_DIM)
    return pl.ds(pl.multiple_of(head * HEAD_DIM, HEAD_DIM), HEAD_DIM)


def rows_of(chunk):
    return slice(chunk * CHUNK, (chunk + 1) * CHUNK)


def bucket_slot(depth_count, depth, chunk):
    before = sum(1 << (depth_count - d - 1) for d in range(depth))
    return before + (((chunk >> depth) - 1) >> 1)


def state_kernel(
    span, pos_ref, k_hbm, v_hbm, q_hbm, w_hbm,
    k_ref, v_ref, local_ref, block_ref, q_ref, w_ref, held, sems, more_sems,
):
    del pos_ref
    rows = k_ref.shape[0]
    heads = block_ref.shape[0]
    chunks = rows // CHUNK
    depth_count = chunks.bit_length() - 1
    copies = []
    for c in range(chunks):
        here = pl.ds(c * CHUNK, CHUNK)
        pair = [
            pltpu.make_async_copy(k_hbm.at[here], k_ref.at[here], sems.at[0, c]),
            pltpu.make_async_copy(v_hbm.at[here], v_ref.at[here], sems.at[1, c]),
        ]
        for copy in pair:
            copy.start()
        copies.append(pair)
    more = [
        weight_copy((0, w_ref.shape[2] // CHUNK), w_hbm, w_ref, more_sems.at[0]),
        query_copy(span, q_hbm, q_ref, more_sems.at[1]),
    ]
    for c in range(chunks):
        for copy in copies[c]:
            copy.wait()
        if c == chunks // 2:
            for copy in more:
                copy.start()
        for h in range(heads):
            state = dot(v_ref[rows_of(c), columns_of(h)], k_ref[rows_of(c), columns_of(h)], LT)
            depth = 0
            while c >> depth & 1:
                state += held[depth, h]
                depth += 1
            if depth < depth_count:
                held[depth, h] = state
                slot = bucket_slot(depth_count, depth, c | (1 << depth))
                local_ref[h, slot] = state.astype(BF16)
            else:
                block_ref[h] = state.astype(BF16)
    for copy in more:
        copy.wait()


def query_copy(span, q_hbm, q_ref, sem):
    here = pl.ds(span[0] * CHUNK, (span[1] - span[0]) * CHUNK)
    return pltpu.make_async_copy(q_hbm.at[here], q_ref, sem)


def weight_copy(span, w_hbm, w_ref, sem):
    here = pl.ds(span[0] * CHUNK, (span[1] - span[0]) * CHUNK)
    return pltpu.make_async_copy(w_hbm.at[:, :, here], w_ref, sem)


def weights_at(w_refs, chunk):
    part = next(p for p in w_refs if p[0] <= chunk < p[1])
    return w_refs[part], (chunk - part[0]) * CHUNK


def sum_kernel(whole, pos_ref, mine_ref, received_ref, after_ref, out_ref):
    del after_ref
    half = out_ref.shape[0]
    here = pl.ds((pos_ref[0] & 1) * half if whole else 0, half)
    total = mine_ref[here].astype(jnp.float32) + received_ref[here].astype(jnp.float32)
    out_ref[...] = total.astype(BF16)


def stack_kernel(*refs):
    out_ref = refs[-1]
    for b, ref in enumerate(refs[:-1]):
        out_ref[b] = ref[...]


def local_factors(w_ref, head, start):
    def row(level):
        return w_ref[head, level : level + 1, start : start + HALF] * SCALING

    groups = HALF // GROUP
    group_id = lax.broadcasted_iota(jnp.int32, (groups, HALF), 0)
    lane_group = lax.broadcasted_iota(jnp.int32, (groups, HALF), 1) >> 3
    apart = group_id ^ lane_group
    coarse = jnp.broadcast_to(row(4), (groups, HALF))
    for level in range(5, 8):
        coarse = jnp.where(apart >= 1 << (level - 4), row(level), coarse)
    coarse = jnp.where(lane_group > group_id, coarse, 0.0)
    sub = lax.broadcasted_iota(jnp.int32, (GROUP, HALF), 0)
    lane = lax.broadcasted_iota(jnp.int32, (GROUP, HALF), 1)
    low = sub ^ (lane & 7)
    fine = jnp.broadcast_to(row(0), (GROUP, HALF))
    for level in range(1, 4):
        fine = jnp.where(low >= 1 << (level - 1), row(level), fine)
    fine = jnp.where(sub <= (lane & 7), fine, 0.0)
    pieces = []
    for g in range(groups):
        wide = jnp.broadcast_to(coarse[g : g + 1, :], (GROUP, HALF))
        pieces.append(jnp.where(lane >> 3 == g, fine, wide))
    return jnp.concatenate(pieces, axis=0)


def local_kernel(
    span, given, loads, w_given, w_loads, lag, first_level, buckets,
    pos_ref, k_ref, v_ref, local_ref, *refs,
):
    refs = list(refs)
    heads = local_ref.shape[0]
    half = heads // 2
    depth_count = (k_ref.shape[0] // CHUNK).bit_length() - 1
    base_level = CHUNK.bit_length()
    bucket_refs = [refs.pop(0) for _ in range(buckets)]
    q_refs = {part: refs.pop(0) for part in given}
    w_refs = {part: refs.pop(0) for part in w_given}
    q_hbm = refs.pop(0) if loads else None
    w_hbm = refs.pop(0) if w_loads else None
    out_ref = refs.pop(0)
    waits = []
    for i, part in enumerate(loads):
        q_refs[part] = refs.pop(0)
        waits.append((part, query_copy(part, q_hbm, q_refs[part], refs[-1].at[i])))
    for part in w_loads:
        w_refs[part] = refs.pop(0)
        copy = weight_copy(part, w_hbm, w_refs[part], refs[-1].at[len(waits)])
        waits.insert(1, (part, copy))
    position = pos_ref[0]
    own = (position & 1) * half

    def arrive():
        waits.pop(0)[1].wait()
        if waits:
            waits[0][1].start()

    if waits:
        waits[0][1].start()

    def scores(c, i, h):
        w_ref, start = weights_at(w_refs, c)
        depths = [d for d in range(depth_count) if c >> d & 1]
        stream = [k_ref[rows_of(c), columns_of(h)]]
        stream += [local_ref[h, bucket_slot(depth_count, d, c)] for d in depths]
        levels = [base_level + d for d in depths]
        for b, ref in enumerate(bucket_refs):
            if b == 0 or i < half:
                state = ref[h] if b == 0 else ref[i]
                present = (position >> b & 1) == 1
                stream.append(jnp.where(present, state, jnp.zeros_like(state)))
                levels.append(first_level + b)
        part = next(p for p in q_refs if p[0] <= c < p[1])
        query = q_refs[part][rows_of(c - part[0]), columns_of(h)]
        result = dot(jnp.concatenate(stream, axis=0), query, TT)
        upper = (result[:HALF, :HALF] * local_factors(w_ref, h, start)).astype(BF16)
        lower = (result[HALF:CHUNK, HALF:] * local_factors(w_ref, h, start + HALF)).astype(BF16)
        middle_row = w_ref[h, 8:9, start + HALF : start + CHUNK] * SCALING
        middle = (result[:HALF, HALF:] * middle_row).astype(BF16)
        weighted = jnp.concatenate(
            [
                jnp.concatenate([upper, middle], axis=1),
                jnp.concatenate([jnp.zeros_like(upper), lower], axis=1),
            ],
            axis=0,
        )
        total = None
        for n, level in enumerate(levels):
            piece = result[CHUNK + n * VALUE_DIM : CHUNK + (n + 1) * VALUE_DIM]
            piece = piece * (w_ref[h, level : level + 1, start : start + CHUNK] * SCALING)
            total = piece if total is None else total + piece
        return weighted, total

    def values(c, h, weighted, total):
        inside = dot(v_ref[rows_of(c), columns_of(h)], weighted, LT)
        if total is not None:
            inside += total
        out_ref[c - span[0], columns_of(h), :] = inside.astype(BF16)

    waiting = []
    for c in range(*span):
        while waits and waits[0][0][0] <= c:
            arrive()
        for i in range(heads):
            h = i
            if buckets > 1:
                h = own + i if i < half else i - own
            waiting.append((c, h, *scores(c, i, h)))
            if len(waiting) > lag:
                values(*waiting.pop(0))
    for entry in waiting:
        values(*entry)
    while waits:
        arrive()


def across_kernel(mine, bits, done, first_level, spans, parts, w_parts, part, pos_ref, *refs):
    refs = list(refs)
    q_refs = {p: refs.pop(0) for p in parts}
    w_refs = {p: refs.pop(0) for p in w_parts}
    in_refs = [refs.pop(0) for _ in spans]
    first_ref = refs.pop(0)
    rest_ref = refs.pop(0) if bits > 1 else None
    mix_ref, square_ref = refs[-2:]
    half = w_refs[w_parts[0]].shape[0] // 2
    position = pos_ref[0]
    own = (position & 1) * half
    first = own if mine else half - own
    squares = {}
    for i in range(half):
        head = first + i
        states = []
        for b in range(bits):
            state = first_ref[head] if b == 0 else rest_ref[b - 1, i]
            states.append(jnp.where((position >> b & 1) == 1, state, jnp.zeros_like(state)))
        for c in range(*part):
            s = [low <= c < high for low, high in spans].index(True)
            local = c - spans[s][0]
            w_ref, start = weights_at(w_refs, c)
            used = range(done[s] if mine else min(done[s], 1), bits)
            place = next(p for p in parts if p[0] <= c < p[1])
            total = in_refs[s][local, columns_of(head), :].astype(jnp.float32)
            if len(used):
                stream = jnp.concatenate([states[b] for b in used], axis=0)
                result = dot(stream, q_refs[place][rows_of(c - place[0]), columns_of(head)], TT)
                for n, b in enumerate(used):
                    level = first_level + b
                    row = w_ref[head, level : level + 1, start : start + CHUNK] * SCALING
                    total += result[n * VALUE_DIM : (n + 1) * VALUE_DIM] * row
            square = jnp.sum((total * total).reshape(VALUE_DIM // GROUP, GROUP, CHUNK), axis=0)
            squares[c] = squares[c] + square if c in squares else square
            mix_ref[rows_of(c - part[0]), columns_of(i)] = total.astype(BF16).T
    for c in range(*part):
        here = rows_of(c - part[0])
        square = jnp.sum(squares[c], axis=0, keepdims=True)
        if not mine:
            square += refs[0][:, rows_of(c)]
        square_ref[:, here] = square


def norm_kernel(
    width, pos_ref, own_ref, other_ref, gain_ref, *refs
):
    *square_refs, out_hbm, out_ref, sems = refs
    rows, half = own_ref.shape
    own = (pos_ref[0] & 1) * half
    step = CHUNK // 2
    slots = out_ref.shape[0] // step
    copies = []
    for i in range(rows // step):
        here = pl.ds(i * step, step)
        slot = pl.ds(i % slots * step, step)
        if i >= slots:
            copies[i - slots].wait()
        square = sum(ref[:, here] for ref in square_refs)
        factor = lax.rsqrt(square / width + 1e-05)
        column = jnp.broadcast_to(factor, (GROUP, step)).T[:, :1]
        for mix_ref, first in ((own_ref, own), (other_ref, half - own)):
            there = pl.ds(pl.multiple_of(first, HEAD_DIM), half)
            mixture = mix_ref[here, :].astype(jnp.float32)
            out_ref[slot, there] = (mixture * gain_ref[:, there] * column).astype(out_ref.dtype)
        copy = pltpu.make_async_copy(out_ref.at[slot], out_hbm.at[here], sems.at[i])
        copy.start()
        copies.append(copy)
    for copy in copies[-slots:]:
        copy.wait()


def body(queries, key_vectors, value_vectors, level_weights, norm_gain):
    rows, columns = queries.shape
    heads = level_weights.shape[0]
    levels = level_weights.shape[1]
    half = heads // 2
    chunks = rows // CHUNK
    depth_count = chunks.bit_length() - 1
    first_level = rows.bit_length()
    seq_size = lax.axis_size("seq")
    head_size = lax.axis_size("head")
    cross_bits = seq_size.bit_length() - 1
    position = lax.axis_index("seq").astype(jnp.int32).reshape(1)
    scalar = pl.BlockSpec(memory_space=pltpu.SMEM)

    def call(kernel, name, operands, out_shape, flops=0, size=0, limit=8, in_specs=None, **settings):
        if in_specs is None:
            in_specs = [scalar] + [WHOLE] * (len(operands) - 1)
        if "out_specs" not in settings:
            settings["out_specs"] = jax.tree.map(lambda _: WHOLE, out_shape)
        return pl.pallas_call(
            kernel,
            name=name,
            in_specs=in_specs,
            out_shape=out_shape,
            compiler_params=pltpu.CompilerParams(vmem_limit_bytes=limit * MIB),
            cost_estimate=pl.CostEstimate(
                flops=int(flops), bytes_accessed=int(size), transcendentals=0
            ),
            **settings,
        )(*operands)

    cuts = sorted({0, chunks // 8, chunks * 5 // 8, chunks})
    spans = list(zip(cuts[:-1], cuts[1:]))
    middle = (spans[1][0] + spans[1][1]) // 2
    parts = [spans[0], (spans[1][0], middle), (middle, spans[1][1]), spans[2]]
    plan = [(parts[:1], parts[1:2]), (parts[1:2], parts[2:]), (parts[3:], [])]
    w_parts = [(0, middle), (middle, chunks)]
    w_plan = [(w_parts[:1], []), (w_parts[:1], w_parts[1:]), (w_parts[1:], [])]
    done = [0, 1, min(2, cross_bits)]

    def weight_shape(span):
        return pltpu.VMEM((heads, levels, (span[1] - span[0]) * CHUNK), jnp.float32)

    def query_shape(span):
        return pltpu.VMEM(((span[1] - span[0]) * CHUNK, columns), BF16)

    per_chunk = 2 * heads * CHUNK * 128 * 128
    queries, level_weights = leave(queries), leave(level_weights)
    keys, values, local_states, block_state, query, weight = call(
        functools.partial(state_kernel, spans[0]),
        "states",
        [position, leave(key_vectors), leave(value_vectors), queries, level_weights],
        [
            pltpu.VMEM((rows, columns), BF16),
            pltpu.VMEM((rows, columns), BF16),
            pltpu.VMEM((heads, chunks - 1, VALUE_DIM, HEAD_DIM), BF16),
            jax.ShapeDtypeStruct((heads, VALUE_DIM, HEAD_DIM), BF16),
        ]
        + [query_shape(spans[0]), weight_shape(w_parts[0])],
        flops=chunks * per_chunk,
        size=4 * rows * columns,
        in_specs=[scalar] + [ANYWHERE] * 4,
        scratch_shapes=[
            pltpu.VMEM((depth_count, heads, VALUE_DIM, HEAD_DIM), jnp.float32),
            pltpu.SemaphoreType.DMA((2, chunks)),
            pltpu.SemaphoreType.DMA((2,)),
        ],
    )
    weights = {w_parts[0]: keep(weight)}
    keys, values, local_states = keep(keys), keep(values), keep(local_states)

    def swap(array, bit):
        return lax.ppermute(array, "seq", [(i, i ^ (1 << bit)) for i in range(seq_size)])

    def add(mine, received, after, whole):
        return call(
            functools.partial(sum_kernel, whole),
            "sum",
            [position, mine, received, after],
            jax.ShapeDtypeStruct((half, VALUE_DIM, HEAD_DIM), BF16),
            limit=4,
            in_specs=[scalar, WHOLE, WHOLE, WHOLE],
        )

    received = swap(block_state, 0)
    buckets = [received]
    running = block_state
    insides = []
    held = {parts[0]: keep(query)}
    for p, span in enumerate(spans):
        count = span[1] - span[0]
        given, loads = plan[p]
        w_given, w_loads = w_plan[p]
        operands = [position, keys, values, local_states]
        operands += buckets[: done[p]] + [held[part] for part in given]
        operands += [weights[part] for part in w_given]
        in_specs = [scalar] + [WHOLE] * (len(operands) - 1)
        out_shape = [pltpu.VMEM((count, columns, CHUNK), BF16)]
        scratch = []
        if loads:
            operands.append(queries)
            in_specs.append(ANYWHERE)
            out_shape += [query_shape(part) for part in loads]
            if w_loads:
                operands.append(level_weights)
                in_specs.append(ANYWHERE)
                out_shape += [weight_shape(part) for part in w_loads]
            scratch = [pltpu.SemaphoreType.DMA((len(loads) + len(w_loads),))]
        results = call(
            functools.partial(
                local_kernel, span, given, loads, w_given, w_loads, 2, first_level, done[p]
            ),
            "local",
            operands,
            out_shape,
            flops=count * per_chunk * 18,
            in_specs=in_specs,
            scratch_shapes=scratch,
        )
        insides.append(keep(results[0]))
        arrays = [keep(array) for array in results[1:]]
        held.update(zip(loads, arrays))
        weights.update(zip(w_loads, arrays[len(loads) :]))
        if p + 1 < cross_bits:
            running = add(running, received, insides[-1], p == 0)
            received = swap(running, p + 1)
            buckets.append(received)
    for b in range(len(spans) + 1, cross_bits):
        running = add(running, received, insides[-1], False)
        received = swap(running, b)
        buckets.append(received)
    own_buckets = other_buckets = buckets[:1]
    if cross_bits > 1:
        own = call(
            stack_kernel,
            "stack",
            buckets[1:],
            jax.ShapeDtypeStruct((cross_bits - 1, half, VALUE_DIM, HEAD_DIM), BF16),
            in_specs=[WHOLE] * (cross_bits - 1),
        )
        own_buckets = buckets[:1] + [own]
        other_buckets = buckets[:1] + [swap(own, 0)]

    shared = [position, *[held[part] for part in parts], *weights.values(), *insides]

    def across(mine, operands):
        return call(
            functools.partial(
                across_kernel, mine, cross_bits, done, first_level, spans, parts, w_parts, (0, chunks)
            ),
            "across",
            operands,
            [
                pltpu.VMEM((rows, columns // 2), BF16),
                jax.ShapeDtypeStruct((1, rows), jnp.float32),
            ],
            flops=chunks * per_chunk * 6,
        )

    own_mix, square = across(True, shared + own_buckets)
    other_mix, square = across(False, shared + other_buckets + [square])
    squares = [square]
    for other in range(1, head_size):
        squares.append(
            lax.ppermute(square, "head", [(i, i ^ other) for i in range(head_size)])
        )
    return call(
        functools.partial(norm_kernel, HEADS * VALUE_DIM),
        "norm",
        [position, keep(own_mix), keep(other_mix), norm_gain.reshape(1, -1), *squares],
        jax.ShapeDtypeStruct((rows, columns), BF16),
        flops=3 * rows * columns,
        size=2 * rows * columns,
        out_specs=ANYWHERE,
        scratch_shapes=[
            pltpu.VMEM((rows // 2, columns), BF16),
            pltpu.SemaphoreType.DMA((2 * chunks,)),
        ],
    )


def solution(mesh):
    placed = (
        P("seq", "head"),
        P("seq", "head"),
        P("seq", "head"),
        P("head", None, "seq"),
        P("head"),
    )
    return jax.shard_map(
        body, mesh=mesh, in_specs=placed, out_specs=P("seq", "head"), check_vma=False
    )
```
